128 devices in a mesh: row: 8 (over y, core), col: 8 (over z, x_hi), smp: 2 (over x_lo).
Axes of the slice: x: 4 (x_hi: 2, x_lo: 2; x = x_hi * 2 + x_lo), y: 4, z: 4, core: 2. Of those that a mesh axis runs over, the one named last changes fastest.
Arguments:
- token_act: bfloat16 [8, 2048, 768], P('smp', ('row', 'col')), may hold values from -9 to 9
- pair_rep: bfloat16 [2048, 2048, 128], P('row', 'col'), may hold values from -4 to 402
- norm_gain: float32 [768], replicated, may hold values from 0.1 to 1.9
- w_pair: bfloat16 [128, 16], replicated, may hold values from -1 to 1
- w_query: bfloat16 [768, 768], P(None, 'col'), may hold values from -0.21875 to 0.21875
- w_key: bfloat16 [768, 768], P(None, 'col'), may hold values from -0.21875 to 0.21875
- w_value: bfloat16 [768, 768], P(None, 'col'), may hold values from -0.21875 to 0.21875
- w_gate: bfloat16 [768, 768], P(None, 'col'), may hold values from -0.21875 to 0.21875
- w_out: bfloat16 [768, 768], P('col'), may hold values from -0.21875 to 0.21875
- grad_out: bfloat16 [8, 2048, 768], P('smp', ('row', 'col')), may hold values from -6 to 6
Outputs:
- block_out: bfloat16 [8, 2048, 768], P('smp', ('row', 'col'))
- grad_act: bfloat16 [8, 2048, 768], P('smp', ('row', 'col'))
- grad_query: float32 [768, 768], P(None, 'col')
- grad_key: float32 [768, 768], P(None, 'col')
- grad_value: float32 [768, 768], P(None, 'col')
- grad_gate: float32 [768, 768], P(None, 'col')
- grad_wout: float32 [768, 768], P('col')
- grad_wpair: float32 [128, 16], replicated
- grad_gain: float32 [768], replicated
The draws below stay inside these ranges and needn't reach their ends.
All inputs are finite; a program needn't handle non-finite values.
Results may differ from the reference program's by a relative error of at most 0.019.
Values may be sent and summed in bfloat16 or wider, within the bound.
No kernel may reach another device: no remote copies, remote signals or barrier semaphores. Data moves between devices by JAX's collectives and lax.ppermute only.
A program may use at most 576 MiB of HBM per device.

```python
import math
import jax
import jax.numpy as jnp
from jax import lax

C = 768
H = 16
CZ = 128
N = 2048
S = 8


def draw_token_act(key, part):
    key = jax.random.fold_in(key, 3)
    key_one, key_two, key_three = jax.random.split(key, 3)
    row_scale = 0.1 * jnp.exp(jax.random.uniform(key_two, (S, N, 1), jnp.float32) * math.log(10.0))
    col_scale = 0.3 * jnp.exp(jax.random.uniform(key_three, (C,), jnp.float32) * math.log(10.0))
    noise = jnp.clip(jax.random.normal(key_one, (S, N, C), jnp.float32), -3.0, 3.0)
    return (noise * row_scale * col_scale).astype(jnp.bfloat16)


def draw_pair_rep(key, part):
    key = jax.random.fold_in(key, 7)
    key_one = jax.random.fold_in(key, 0)
    base = jnp.clip(jax.random.normal(key_one, (N, N, CZ), jnp.float32), -4.0, 4.0)
    return base.astype(jnp.bfloat16)


def block_scale(rng, extent, cuts, low, largest):
    def one(position, shards_of):
        steps = jax.random.uniform(jax.random.fold_in(jax.random.fold_in(rng, 6), position), (shards_of,), jnp.float32, low / len(cuts), largest / len(cuts))
        return jnp.repeat(jnp.exp(steps), extent[position] // shards_of).reshape((-1,) + (1,) * (len(extent) - position - 1))

    loudness = one(*cuts[0])
    for cut in cuts[1:]:
        loudness = loudness * one(*cut)
    return loudness


def normal_values(own_key, shape, spread, reach, cuts=(), held_as=jnp.bfloat16):
    values = spread * jax.random.normal(own_key, shape, jnp.float32)
    if cuts:
        values = values * block_scale(own_key, shape, cuts, -0.22, 0.18)
    return jnp.clip(values, -reach, reach).astype(held_as)


def setup_inputs(seed: int = 0) -> dict:
    seeds = jax.random.split(jax.random.key(seed), 11)
    return {
        "token_act": draw_token_act(jax.random.fold_in(seeds[10], 71), 0),
        "pair_rep": draw_pair_rep(jax.random.fold_in(seeds[10], 71), 0),
        "norm_gain": jnp.clip(1.0 + 0.18 * jax.random.normal(seeds[2], (C,), jnp.float32), 0.1, 1.9),
        "w_pair": normal_values(seeds[3], (CZ, H), (CZ // 4) ** -0.5, 1.0),
        "w_query": normal_values(seeds[4], (C, C), C ** -0.5, 0.21875, ((1, 8),)),
        "w_key": normal_values(seeds[5], (C, C), C ** -0.5, 0.21875, ((1, 8),)),
        "w_value": normal_values(seeds[6], (C, C), C ** -0.5, 0.21875, ((1, 8),)),
        "w_gate": normal_values(seeds[7], (C, C), C ** -0.5, 0.21875, ((1, 8),)),
        "w_out": normal_values(seeds[8], (C, C), C ** -0.5, 0.21875, ((0, 8),)),
        "grad_out": normal_values(seeds[9], (S, N, C), 1.0, 6.0, ((0, 2), (1, 64))),
    }


EPSILON = 1e-05

def normalize(token_act, norm_gain):
    values_f = token_act.astype(jnp.float32)
    centred = values_f - lax.optimization_barrier(jnp.mean(values_f, axis=-1, keepdims=True))
    inv_std = lax.rsqrt(lax.optimization_barrier(jnp.mean(centred * centred, axis=-1, keepdims=True)) + EPSILON)
    normed = centred * inv_std
    return ((normed * norm_gain).astype(jnp.bfloat16), normed, inv_std)

def normalize_back(grad_norm, normed, inv_std, norm_gain):
    grad_hat = grad_norm * norm_gain
    return inv_std * (grad_hat - lax.optimization_barrier(jnp.mean(grad_hat, axis=-1, keepdims=True)) - normed * lax.optimization_barrier(jnp.mean(grad_hat * normed, axis=-1, keepdims=True)))

def reference(token_act, pair_rep, norm_gain, w_pair, w_query, w_key, w_value, w_gate, w_out, grad_out):
    samples, length, width = token_act.shape
    heads = w_pair.shape[1]
    head_dim = width // heads
    channels = pair_rep.shape[2]
    score_scale = 1.0 / math.sqrt(head_dim)
    block = math.gcd(length, 64)
    pair_blocks = pair_rep.reshape(length // block, block, length, channels)
    bias_blocks = lax.map(lambda piece: jnp.einsum('ijc,ch->hij', piece.astype(jnp.float32), w_pair.astype(jnp.float32)), pair_blocks)
    bias = jnp.moveaxis(bias_blocks, 0, 1).reshape(heads, length, length)
    token_norm, normed, inv_std = normalize(token_act, norm_gain)
    flat_norm = token_norm.reshape(samples * length, width)

    def project(weight):
        return jnp.dot(flat_norm, weight, preferred_element_type=jnp.float32).astype(jnp.bfloat16).reshape(samples, length, width)
    queries = project(w_query)
    keys_all = project(w_key)
    values_all = project(w_value)
    gates = project(w_gate)

    def one_sample(grad_bias, inputs):
        query_s, key_s, value_s, gate_s, cot_s = inputs
        query_h = query_s.reshape(length, heads, head_dim).astype(jnp.float32)
        key_h = key_s.reshape(length, heads, head_dim).astype(jnp.float32)
        value_h = value_s.reshape(length, heads, head_dim).astype(jnp.float32)
        scores = jnp.einsum('ihd,jhd->hij', query_h, key_h) * score_scale + bias
        peak = lax.optimization_barrier(jnp.max(scores, axis=-1, keepdims=True))
        expo = jnp.exp(scores - peak)
        probs = expo / lax.optimization_barrier(jnp.sum(expo, axis=-1, keepdims=True))
        probs_bf = probs.astype(jnp.bfloat16)
        attended = jnp.einsum('hij,jhd->ihd', probs_bf.astype(jnp.float32), value_h).reshape(length, width)
        gate_sig = jax.nn.sigmoid(gate_s.astype(jnp.float32))
        gated = (gate_sig * attended).astype(jnp.bfloat16)
        grad_gated = jnp.dot(cot_s, w_out.T, preferred_element_type=jnp.float32).astype(jnp.bfloat16)
        grad_gf = grad_gated.astype(jnp.float32)
        grad_att = (grad_gf * gate_sig).astype(jnp.bfloat16)
        grad_gpre = (grad_gf * attended * gate_sig * (1.0 - gate_sig)).astype(jnp.bfloat16)
        grad_ah = grad_att.reshape(length, heads, head_dim).astype(jnp.float32)
        grad_probs = jnp.einsum('ihd,jhd->hij', grad_ah, value_h)
        row_dot = lax.optimization_barrier(jnp.sum(probs * grad_probs, axis=-1, keepdims=True))
        grad_scores = (probs * (grad_probs - row_dot)).astype(jnp.bfloat16).astype(jnp.float32)
        grad_q = (jnp.einsum('hij,jhd->ihd', grad_scores, key_h) * score_scale).astype(jnp.bfloat16).reshape(length, width)
        grad_k = (jnp.einsum('hij,ihd->jhd', grad_scores, query_h) * score_scale).astype(jnp.bfloat16).reshape(length, width)
        grad_v = jnp.einsum('hij,ihd->jhd', probs_bf.astype(jnp.float32), grad_ah).astype(jnp.bfloat16).reshape(length, width)
        return (grad_bias + grad_scores, (gated, grad_q, grad_k, grad_v, grad_gpre))
    grad_bias, stacked = lax.scan(one_sample, jnp.zeros((heads, length, length), jnp.float32), (queries, keys_all, values_all, gates, grad_out))
    gated, grad_q, grad_k, grad_v, grad_gpre = stacked
    gated_flat = gated.reshape(samples * length, width)
    cot_flat = grad_out.reshape(samples * length, width)
    out_sum = jnp.dot(gated_flat, w_out, preferred_element_type=jnp.float32).reshape(samples, length, width)
    block_out = (token_act.astype(jnp.float32) + out_sum).astype(jnp.bfloat16)
    grad_wout = jnp.dot(gated_flat.T, cot_flat, preferred_element_type=jnp.float32)
    grad_list = [grad_q, grad_k, grad_v, grad_gpre]
    weight_list = [w_query, w_key, w_value, w_gate]
    weight_grads = []
    grad_norm = jnp.zeros((samples * length, width), jnp.float32)
    for grad_part, weight in zip(grad_list, weight_list):
        grad_flat = grad_part.reshape(samples * length, width)
        weight_grads.append(jnp.dot(flat_norm.T, grad_flat, preferred_element_type=jnp.float32))
        grad_norm = grad_norm + jnp.dot(grad_flat, weight.T, preferred_element_type=jnp.float32)
    grad_norm = grad_norm.reshape(samples, length, width)
    grad_gain = lax.optimization_barrier(jnp.sum(grad_norm * normed, axis=(0, 1)))
    grad_act = (grad_out.astype(jnp.float32) + normalize_back(grad_norm, normed, inv_std, norm_gain)).astype(jnp.bfloat16)
    grad_blocks = jnp.moveaxis(grad_bias.reshape(heads, length // block, block, length), 1, 0)

    def add_block(total, pieces):
        pair_piece, grad_piece = pieces
        return (total + jnp.einsum('ijc,hij->ch', pair_piece.astype(jnp.float32), grad_piece, precision=lax.Precision.HIGHEST), None)
    grad_wpair, _ = lax.scan(add_block, jnp.zeros((channels, heads), jnp.float32), (pair_blocks, grad_blocks))
    return (block_out, grad_act, weight_grads[0], weight_grads[1], weight_grads[2], weight_grads[3], grad_wout, grad_wpair, grad_gain)
```

```python
import functools
import math

import jax
import jax.numpy as jnp
from jax import lax
from jax.experimental import pallas as pl
from jax.experimental.pallas import tpu as pltpu
from jax.sharding import Mesh, PartitionSpec as P

EPSILON = 1e-05
BF = jnp.bfloat16
F32 = jnp.float32
HD = 48
COL = ("z", "xh")
ROW = ("y", "core")
GROUP = ("y", "core", "smp")

NT = (((1,), (1,)), ((), ()))
NN = (((1,), (0,)), ((), ()))
TN = (((0,), (0,)), ((), ()))


def mm(a, b, dims):
    return lax.dot_general(a, b, dims, preferred_element_type=F32)


BIAS_ROWS = 2 * 256 + 16


def bias_kernel(w_ref, pair_ref, out_ref, acc_ref):
    heads, rows, keys = acc_ref.shape
    for block in range(rows // 16):
        piece = jnp.concatenate([pair_ref[block * 16 + k] for k in range(16)], axis=1)
        res = mm(w_ref[...], piece, NT)
        acc_ref[:, block * 16 : (block + 1) * 16, :] = res.reshape(heads, 16, keys)
    row_id = lax.broadcasted_iota(jnp.int32, (16, rows), 0)
    for group in range(heads // 2):
        tops = jnp.zeros((16, rows), F32)
        for half in range(2):
            tile = acc_ref[group * 2 + half].T
            top = jnp.max(tile, axis=0, keepdims=True)
            out_ref[group, half * keys : (half + 1) * keys, :] = (tile - top).astype(BF)
            one = top.astype(BF).astype(F32)
            two = (top - one).astype(BF).astype(F32)
            for k, term in enumerate((one, two, top - one - two)):
                tops = jnp.where(row_id == half * 3 + k, term, tops)
        out_ref[group, 2 * keys :, :] = tops.astype(BF)


def pair_bias(pair, w_pair):
    rows, keys, chans = pair.shape
    heads = w_pair.shape[1]
    eye = jnp.eye(16, dtype=BF)
    spread = (w_pair.T[:, None, None, :] * eye[None, :, :, None]).reshape(heads * 16, 16 * chans)
    step = 128
    return pl.pallas_call(
        bias_kernel,
        grid=(rows // step,),
        in_specs=[
            pl.BlockSpec(spread.shape, lambda i: (0, 0)),
            pl.BlockSpec((step, keys, chans), lambda i: (i, 0, 0)),
        ],
        out_specs=pl.BlockSpec((heads // 2, BIAS_ROWS, step), lambda i: (0, 0, i)),
        out_shape=jax.ShapeDtypeStruct((heads // 2, BIAS_ROWS, rows), BF),
        scratch_shapes=[pltpu.VMEM((heads, step, keys), F32)],
        compiler_params=pltpu.CompilerParams(vmem_limit_bytes=44 * 2**20),
        cost_estimate=pl.CostEstimate(flops=2**32, bytes_accessed=20 * 2**20, transcendentals=0),
        name="pair_bias",
    )(spread, pair)


def project_kernel(rows_ref, wq_ref, wk_ref, wv_ref, wg_ref, q_ref, kv_ref, g_ref):
    rows = rows_ref[:, 0].reshape(256, rows_ref.shape[-1])
    q_ref[0] = mm(wq_ref[...], rows, NT).astype(BF)
    g_ref[0] = mm(wg_ref[...], rows, NT).astype(BF)
    keys = mm(wk_ref[...], rows, NT).astype(BF)
    values = mm(wv_ref[...], rows, NT).astype(BF)
    for h in range(2):
        kv_ref[0, h, :HD, :] = keys[h * HD : (h + 1) * HD, :]
        kv_ref[0, h, HD:, :] = values[h * HD : (h + 1) * HD, :]


def project(rows_in, wq, wk, wv, wg):
    cols, samples, local, width = rows_in.shape
    feat = wq.shape[0]
    tok = cols * local
    wspec = pl.BlockSpec((feat, width), lambda s: (0, 0))
    small = jax.ShapeDtypeStruct((samples, feat, tok), BF)
    small_spec = pl.BlockSpec((1, feat, tok), lambda s: (s, 0, 0))
    return pl.pallas_call(
        project_kernel,
        grid=(samples,),
        in_specs=[pl.BlockSpec((cols, 1, local, width), lambda s: (0, s, 0, 0))] + [wspec] * 4,
        out_specs=[small_spec, pl.BlockSpec((1, 2, feat, tok), lambda s: (s, 0, 0, 0)), small_spec],
        out_shape=[small, jax.ShapeDtypeStruct((samples, 2, feat, tok), BF), small],
        compiler_params=pltpu.CompilerParams(vmem_limit_bytes=24 * 2**20),
        name="project",
    )(rows_in, wq, wk, wv, wg)


def gated_grad_kernel(rows_ref, w_ref, out_ref):
    rows = rows_ref[:, 0].reshape(256, rows_ref.shape[-1])
    out_ref[0] = mm(w_ref[...], rows, NT).astype(BF)


def gated_grad(grad_rows, w_out):
    cols, samples, local, width = grad_rows.shape
    feat = w_out.shape[0]
    tok = cols * local
    return pl.pallas_call(
        gated_grad_kernel,
        grid=(samples,),
        in_specs=[
            pl.BlockSpec((cols, 1, local, width), lambda s: (0, s, 0, 0)),
            pl.BlockSpec((feat, width), lambda s: (0, 0)),
        ],
        out_specs=pl.BlockSpec((1, feat, tok), lambda s: (s, 0, 0)),
        out_shape=jax.ShapeDtypeStruct((samples, feat, tok), BF),
        compiler_params=pltpu.CompilerParams(vmem_limit_bytes=24 * 2**20),
        name="gated_grad",
    )(grad_rows, w_out)


def slot_xor(t):
    return 2 * (t % 4) + t // 4


def attend_kernel(me_ref, bias_ref, q_ref, gate_ref, gg_ref, *refs):
    kv_refs = refs[:8]
    gated_ref, dq_ref, dgate_ref, dkv_own_ref, dkv_far_ref, dbias_ref = refs[8:14]
    s_scr, dp_scr, db_scr = refs[14:]
    head = pl.program_id(0)
    sample = pl.program_id(1)
    me = me_ref[0]
    scale = 1.0 / math.sqrt(HD)
    q = q_ref[0]
    gg = gg_ref[0].astype(F32)
    sig = 1.0 / (1.0 + jnp.exp(-gate_ref[0].astype(F32)))
    gatt = (gg * sig).astype(BF)
    row_id = lax.broadcasted_iota(jnp.int32, (16, 256), 0)
    wanted = (row_id >= head * 3) & (row_id < head * 3 + 3)

    @pl.when(sample == 0)
    def _():
        db_scr[...] = jnp.zeros_like(db_scr)

    peak = None
    for t in range(8):
        block = me ^ slot_xor(t)
        k = kv_refs[t][0, 0, :HD, :]
        tops = bias_ref[block, 512:528, :].astype(F32)
        top = jnp.sum(jnp.where(wanted, tops, 0.0), axis=0, keepdims=True)
        bias = bias_ref[block, pl.ds(pl.multiple_of(head * 256, 256), 256), :].astype(F32) + top
        score = mm(k, q, TN) * scale + bias
        s_scr[t] = score
        high = jnp.max(score, axis=0, keepdims=True)
        peak = high if peak is None else jnp.maximum(peak, high)
    total = jnp.zeros((1, 256), F32)
    dot = jnp.zeros((1, 256), F32)
    for t in range(8):
        v = kv_refs[t][0, 0, HD:, :]
        e = jnp.exp(s_scr[t] - peak)
        s_scr[t] = e
        dp = mm(v, gatt, TN)
        dp_scr[t] = dp
        total = total + jnp.sum(e, axis=0, keepdims=True)
        dot = dot + jnp.sum(e * dp, axis=0, keepdims=True)
    inv = 1.0 / total
    dot = dot * inv
    att = jnp.zeros((HD, 256), F32)
    dq = jnp.zeros((HD, 256), F32)
    for t in range(8):
        block = me ^ slot_xor(t)
        k = kv_refs[t][0, 0, :HD, :]
        v = kv_refs[t][0, 0, HD:, :]
        prob = s_scr[t] * inv
        prob_bf = prob.astype(BF)
        ds = (prob * (dp_scr[t] - dot)).astype(BF)
        db_scr[block] = db_scr[block] + ds.astype(F32)
        att = att + mm(v, prob_bf, NN)
        dq = dq + mm(k, ds, NN)
        out_ref = dkv_own_ref if t < 4 else dkv_far_ref
        out_ref[t % 4, 0, 0, :HD, :] = (mm(q, ds, NT) * scale).astype(BF)
        out_ref[t % 4, 0, 0, HD:, :] = mm(gatt, prob_bf, NT).astype(BF)
    gated_ref[0] = (sig * att).astype(BF)
    dgate_ref[0] = (gg * att * sig * (1.0 - sig)).astype(BF)
    dq_ref[0] = (dq * scale).astype(BF)

    @pl.when(sample == pl.num_programs(1) - 1)
    def _():
        for t in range(8):
            dbias_ref[t, 0] = db_scr[t].astype(BF)


def attend(me, bias, q, gate, gg, kv):
    samples, feat, tok = q.shape
    heads = 2
    half = pl.BlockSpec((1, HD, tok), lambda h, s: (s, h, 0))
    kv_spec = pl.BlockSpec((1, 1, feat, tok), lambda h, s: (s, h, 0, 0))
    small = jax.ShapeDtypeStruct((samples, feat, tok), BF)
    dkv = jax.ShapeDtypeStruct((4, samples, heads, feat, tok), BF)
    dkv_spec = pl.BlockSpec((4, 1, 1, feat, tok), lambda h, s: (0, s, h, 0, 0))
    return pl.pallas_call(
        attend_kernel,
        grid=(heads, samples),
        in_specs=[
            pl.BlockSpec(memory_space=pltpu.SMEM),
            pl.BlockSpec(bias.shape, lambda h, s: (0, 0, 0)),
            half,
            half,
            half,
        ]
        + [kv_spec] * 8,
        out_specs=[
            half,
            half,
            half,
            dkv_spec,
            dkv_spec,
            pl.BlockSpec((8, 1, 256, tok), lambda h, s: (0, h, 0, 0)),
        ],
        out_shape=[small, small, small, dkv, dkv, jax.ShapeDtypeStruct((8, heads, 256, tok), BF)],
        scratch_shapes=[pltpu.VMEM((8, 256, tok), F32)] * 3,
        compiler_params=pltpu.CompilerParams(vmem_limit_bytes=40 * 2**20),
        cost_estimate=pl.CostEstimate(
            flops=2**34, bytes_accessed=20 * 2**20, transcendentals=2**22
        ),
        name="attend",
    )(me, bias, q, gate, gg, *kv)


def output_kernel(gated_ref, rows_ref, w_ref, part_ref, grad_ref):
    gated = gated_ref[0]
    rows = rows_ref[:, 0].reshape(256, rows_ref.shape[-1])
    part = mm(gated, w_ref[...], TN).astype(BF)
    part_ref[:, 0] = part.reshape(part_ref.shape[0], part_ref.shape[2], part_ref.shape[3])
    grad = mm(gated, rows, NN)

    @pl.when(pl.program_id(0) == 0)
    def _():
        grad_ref[...] = grad

    @pl.when(pl.program_id(0) > 0)
    def _():
        grad_ref[...] += grad


def output_part(gated, grad_rows, w_out):
    cols, samples, local, width = grad_rows.shape
    feat = w_out.shape[0]
    row_spec = pl.BlockSpec((cols, 1, local, width), lambda s: (0, s, 0, 0))
    return pl.pallas_call(
        output_kernel,
        grid=(samples,),
        in_specs=[
            pl.BlockSpec((1, feat, cols * local), lambda s: (s, 0, 0)),
            row_spec,
            pl.BlockSpec((feat, width), lambda s: (0, 0)),
        ],
        out_specs=[row_spec, pl.BlockSpec((feat, width), lambda s: (0, 0))],
        out_shape=[
            jax.ShapeDtypeStruct(grad_rows.shape, BF),
            jax.ShapeDtypeStruct((feat, width), F32),
        ],
        compiler_params=pltpu.CompilerParams(vmem_limit_bytes=24 * 2**20),
        name="output_part",
    )(gated, grad_rows, w_out)


def weights_kernel(dq_ref, dg_ref, *refs):
    kv_refs = refs[:4]
    rows_ref, w_ref, gain_ref, part_ref, grad_ref, gain_out_ref = refs[4:]
    dkv = kv_refs[0][0, 0].astype(F32)
    for ref in kv_refs[1:]:
        dkv = dkv + ref[0, 0].astype(F32)
    dkv = dkv.astype(BF)
    dcat = jnp.concatenate(
        [
            dq_ref[0],
            dkv[0, :HD],
            dkv[1, :HD],
            dkv[0, HD:],
            dkv[1, HD:],
            dg_ref[0],
        ],
        axis=0,
    )
    rows = rows_ref[:, 0].reshape(256, rows_ref.shape[-1])
    part = mm(dcat, w_ref[...], TN).astype(BF)
    part_ref[:, 0] = part.reshape(part_ref.shape[0], part_ref.shape[2], part_ref.shape[3])
    grad = mm(dcat, rows, NN)

    @pl.when(pl.program_id(0) == 0)
    def _():
        grad_ref[...] = grad

    @pl.when(pl.program_id(0) > 0)
    def _():
        grad_ref[...] += grad

    @pl.when(pl.program_id(0) == pl.num_programs(0) - 1)
    def _():
        both = jnp.sum(grad_ref[...] * w_ref[...].astype(F32), axis=0, keepdims=True)
        gain_out_ref[...] = both / gain_ref[...]


def weight_part(dq, dg, kv_pieces, rows_in, w_cat, gain):
    cols, samples, local, width = rows_in.shape
    feat = dq.shape[1]
    tok = cols * local
    row_spec = pl.BlockSpec((cols, 1, local, width), lambda s: (0, s, 0, 0))
    half = pl.BlockSpec((1, feat, tok), lambda s: (s, 0, 0))
    kv_spec = pl.BlockSpec((1, 1, 2, feat, tok), lambda s: (0, s, 0, 0, 0))
    full = pl.BlockSpec(w_cat.shape, lambda s: (0, 0))
    line = pl.BlockSpec((1, width), lambda s: (0, 0))
    return pl.pallas_call(
        weights_kernel,
        grid=(samples,),
        in_specs=[half, half] + [kv_spec] * 4 + [row_spec, full, line],
        out_specs=[row_spec, full, line],
        out_shape=[
            jax.ShapeDtypeStruct(rows_in.shape, BF),
            jax.ShapeDtypeStruct(w_cat.shape, F32),
            jax.ShapeDtypeStruct((1, width), F32),
        ],
        compiler_params=pltpu.CompilerParams(vmem_limit_bytes=32 * 2**20),
        name="weight_part",
    )(dq, dg, *kv_pieces, rows_in, w_cat, gain)


def wpair_kernel(db_ref, pair_ref, out_ref, db_scr, acc_ref):
    step = pair_ref.shape[0]
    chans = pair_ref.shape[2]
    heads = db_scr.shape[0]

    @pl.when(pl.program_id(0) == 0)
    def _():
        acc_ref[...] = jnp.zeros_like(acc_ref)

    for h in range(heads):
        db_scr[h] = db_ref[h // 2, h % 2].astype(F32).T.astype(BF)
    for block in range(step // 16):
        left = db_scr[:, block * 16 : (block + 1) * 16, :].reshape(heads * 16, db_scr.shape[2])
        for k in range(0, 16, 2):
            pair = jnp.concatenate(
                [pair_ref[block * 16 + k], pair_ref[block * 16 + k + 1]], axis=1
            )
            at = slice(k * chans, (k + 2) * chans)
            acc_ref[:, at] += mm(left, pair, NN)

    @pl.when(pl.program_id(0) == pl.num_programs(0) - 1)
    def _():
        total = jnp.zeros((heads, chans), F32)
        row_id = lax.broadcasted_iota(jnp.int32, (heads, 16, chans), 1)
        for k in range(16):
            piece = acc_ref[:, k * chans : (k + 1) * chans].reshape(heads, 16, chans)
            total = total + jnp.sum(jnp.where(row_id == k, piece, 0.0), axis=1)
        out_ref[...] = total


def wpair_part(dbias, pair):
    groups, per, keys, rows = dbias.shape
    heads = groups * per
    chans = pair.shape[2]
    step = 128
    return pl.pallas_call(
        wpair_kernel,
        grid=(rows // step,),
        in_specs=[
            pl.BlockSpec((groups, per, keys, step), lambda i: (0, 0, 0, i)),
            pl.BlockSpec((step, keys, chans), lambda i: (i, 0, 0)),
        ],
        out_specs=pl.BlockSpec((heads, chans), lambda i: (0, 0)),
        out_shape=jax.ShapeDtypeStruct((heads, chans), F32),
        scratch_shapes=[
            pltpu.VMEM((heads, step, keys), BF),
            pltpu.VMEM((heads * 16, 16 * chans), F32),
        ],
        compiler_params=pltpu.CompilerParams(vmem_limit_bytes=44 * 2**20),
        cost_estimate=pl.CostEstimate(flops=2**32, bytes_accessed=20 * 2**20, transcendentals=0),
        name="wpair_part",
    )(dbias, pair)


def exchange(x, axes):
    return lax.all_to_all(x, axes, 0, 0, tiled=True)


def gather(x, axes, count):
    return exchange(jnp.broadcast_to(x[None], (count,) + x.shape), axes)


def swap(x, axis, count, k):
    return lax.ppermute(x, axis, [(i, i ^ k) for i in range(count)])


def on_device(
    token_act, pair_rep, norm_gain, w_pair, w_query, w_key, w_value, w_gate, w_out, grad_out
):
    samples, local, width = token_act.shape
    cols = 8
    me = lax.axis_index("y") * 2 + lax.axis_index("core")

    values_f = token_act.astype(F32)
    centred = values_f - jnp.mean(values_f, axis=-1, keepdims=True)
    inv_std = lax.rsqrt(jnp.mean(centred * centred, axis=-1, keepdims=True) + EPSILON)
    normed = centred * inv_std
    token_norm = (normed * norm_gain).astype(BF)

    rows_in = gather(token_norm, COL, cols)
    bias = exchange(pair_bias(pair_rep, w_pair), COL)
    grad_rows = gather(grad_out, COL, cols)

    wq, wk, wv, wg = w_query.T, w_key.T, w_value.T, w_gate.T
    q, kv_own, gate = project(rows_in, wq, wk, wv, wg)
    near = [kv_own] + [swap(kv_own, "y", 4, k) for k in range(1, 4)]
    far = [swap(x, "core", 2, 1) for x in near]
    gg = gated_grad(grad_rows, w_out)

    gated, dq, dgate, dkv_own, dkv_far, dbias = attend(
        jnp.full((1,), me, jnp.int32), bias, q, gate, gg, near + far
    )
    dkv_far = swap(dkv_far, "core", 2, 1)
    dbias = exchange(dbias, COL)
    out_part, grad_wout = output_part(gated, grad_rows, w_out)
    out_recv = exchange(out_part, COL)

    dkv = (dkv_own.astype(F32) + dkv_far.astype(F32)).astype(BF)
    pieces = [dkv[0:1]] + [swap(dkv[k : k + 1], "y", 4, k) for k in range(1, 4)]
    w_cat = jnp.concatenate([wq, wk, wv, wg], axis=0)
    norm_part, grad_cat, gain_part = weight_part(
        dq, dgate, pieces, rows_in, w_cat, norm_gain[None, :]
    )
    norm_recv = exchange(norm_part, COL)

    grads = jnp.concatenate([grad_cat, grad_wout], axis=0).astype(BF)
    grads = exchange(grads.reshape(16, 30, width), GROUP)
    grads = jnp.sum(grads.astype(F32), axis=0).astype(BF)
    grads = gather(grads, GROUP, 16).reshape(480, width).astype(F32)

    wpair = wpair_part(dbias, pair_rep)
    tiny = jnp.concatenate([wpair.reshape(16, 128), gain_part.reshape(6, 128)], axis=0)
    tiny = jnp.sum(gather(tiny, COL, cols), axis=0)
    tiny = jnp.sum(gather(tiny, GROUP, 16), axis=0)
    grad_wpair = tiny[:16].T
    grad_gain = tiny[16:].reshape(width)

    block_out = (values_f + jnp.sum(out_recv.astype(F32), axis=0)).astype(BF)
    grad_norm = jnp.sum(norm_recv.astype(F32), axis=0)
    grad_hat = grad_norm * norm_gain
    grad_act = grad_out.astype(F32) + inv_std * (
        grad_hat
        - jnp.mean(grad_hat, axis=-1, keepdims=True)
        - normed * jnp.mean(grad_hat * normed, axis=-1, keepdims=True)
    )
    feat = w_out.shape[0]
    return (
        block_out,
        grad_act.astype(BF),
        grads[0:feat].T,
        grads[feat : 2 * feat].T,
        grads[2 * feat : 3 * feat].T,
        grads[3 * feat : 4 * feat].T,
        grads[4 * feat :],
        grad_wpair,
        grad_gain,
    )


def solution(mesh):
    fine = Mesh(mesh.devices.reshape(4, 2, 4, 2, 2), ("y", "core", "z", "xh", "smp"))
    tokens = P("smp", ROW + COL, None)
    split_last = P(None, COL)
    return jax.shard_map(
        on_device,
        mesh=fine,
        in_specs=(
            tokens,
            P(ROW, COL, None),
            P(),
            P(),
            split_last,
            split_last,
            split_last,
            split_last,
            P(COL, None),
            tokens,
        ),
        out_specs=(
            tokens,
            tokens,
            split_last,
            split_last,
            split_last,
            split_last,
            P(COL, None),
            P(),
            P(),
        ),
        check_vma=False,
    )
```

```python
import functools
import math

import jax
import jax.numpy as jnp
from jax import lax
from jax.experimental import pallas as pl
from jax.experimental.pallas import tpu as pltpu
from jax.sharding import Mesh, PartitionSpec as P

EPSILON = 1e-05
BF = jnp.bfloat16
F32 = jnp.float32
HD = 48
VMEM = 56 * 2**20
COL = ("z", "xh")
ROW = ("y", "core")
GROUP = ("y", "core", "smp")

NT = (((1,), (1,)), ((), ()))
NN = (((1,), (0,)), ((), ()))
TN = (((0,), (0,)), ((), ()))


def mm(a, b, dims):
    return lax.dot_general(a, b, dims, preferred_element_type=F32)


GG_ROWS = 64
TOP_AT = GG_ROWS + 2 * 256
BIAS_ROWS = TOP_AT + 16


def bias_kernel(w_ref, pair_ref, out_ref, acc_ref):
    heads, rows, keys = acc_ref.shape
    for block in range(rows // 16):
        piece = jnp.concatenate([pair_ref[block * 16 + k] for k in range(16)], axis=1)
        res = mm(w_ref[...], piece, NT)
        acc_ref[:, block * 16 : (block + 1) * 16, :] = res.reshape(heads, 16, keys)
    row_id = lax.broadcasted_iota(jnp.int32, (16, rows), 0)
    for group in range(heads // 2):
        tops = jnp.zeros((16, rows), F32)
        for half in range(2):
            tile = acc_ref[group * 2 + half].T
            top = jnp.max(tile, axis=0, keepdims=True)
            at = GG_ROWS + half * keys
            out_ref[group, at : at + keys, :] = (tile - top).astype(BF)
            one = top.astype(BF).astype(F32)
            two = (top - one).astype(BF).astype(F32)
            for k, term in enumerate((one, two, top - one - two)):
                tops = jnp.where(row_id == half * 3 + k, term, tops)
        out_ref[group, TOP_AT:, :] = tops.astype(BF)


def pair_bias(pair, w_pair):
    rows, keys, chans = pair.shape
    heads = w_pair.shape[1]
    eye = jnp.eye(16, dtype=BF)
    spread = (w_pair.T[:, None, None, :] * eye[None, :, :, None]).reshape(heads * 16, 16 * chans)
    step = 128
    return pl.pallas_call(
        bias_kernel,
        grid=(rows // step,),
        in_specs=[
            pl.BlockSpec(spread.shape, lambda i: (0, 0)),
            pl.BlockSpec((step, keys, chans), lambda i: (i, 0, 0)),
        ],
        out_specs=pl.BlockSpec((heads // 2, BIAS_ROWS, step), lambda i: (0, 0, i)),
        out_shape=jax.ShapeDtypeStruct((heads // 2, BIAS_ROWS, rows), BF),
        scratch_shapes=[pltpu.VMEM((heads, step, keys), F32)],
        compiler_params=pltpu.CompilerParams(vmem_limit_bytes=VMEM),
        cost_estimate=pl.CostEstimate(flops=2**34, bytes_accessed=2**25, transcendentals=0),
        name="pair_bias",
    )(spread, pair)


def prepare_kernel(core_ref, act_ref, gain_ref, w_ref, out_ref):
    samples, local, width = act_ref.shape
    act = act_ref[...].reshape(samples * local, width).astype(F32)
    centred = act - jnp.mean(act, axis=-1, keepdims=True)
    inv_std = lax.rsqrt(jnp.mean(centred * centred, axis=-1, keepdims=True) + EPSILON)
    norm = (centred * inv_std * gain_ref[...]).astype(BF)
    half = w_ref[pl.ds(pl.multiple_of(core_ref[0] * HD, 16), HD), :]
    for c in range(out_ref.shape[0]):
        out_ref[c, : samples * local, :] = norm
        out_ref[c, samples * local :, :] = half


def prepare(core, token_act, gain, w_out, cols):
    samples, local, width = token_act.shape
    vmem = pl.BlockSpec(memory_space=pltpu.VMEM)
    return pl.pallas_call(
        prepare_kernel,
        in_specs=[pl.BlockSpec(memory_space=pltpu.SMEM), vmem, vmem, vmem],
        out_shape=jax.ShapeDtypeStruct((cols, samples * local + HD, width), BF),
        compiler_params=pltpu.CompilerParams(vmem_limit_bytes=VMEM),
        name="prepare",
    )(core, token_act, gain, w_out)


def project_kernel(rows_ref, wq_ref, wk_ref, wv_ref, wg_ref, q_ref, kv_ref, g_ref):
    rows = rows_ref[...].reshape(256, rows_ref.shape[-1])
    q_ref[0] = mm(wq_ref[...], rows, NT).astype(BF)
    g_ref[0] = mm(wg_ref[...], rows, NT).astype(BF)
    keys = mm(wk_ref[...], rows, NT).astype(BF)
    values = mm(wv_ref[...], rows, NT).astype(BF)
    for h in range(2):
        kv_ref[0, h, :HD, :] = keys[h * HD : (h + 1) * HD, :]
        kv_ref[0, h, HD:, :] = values[h * HD : (h + 1) * HD, :]


def project(rows_in, samples, local, wq, wk, wv, wg):
    cols, _, width = rows_in.shape
    feat = wq.shape[0]
    tok = cols * local
    wspec = pl.BlockSpec((feat, width), lambda s: (0, 0))
    small = jax.ShapeDtypeStruct((samples, feat, tok), BF)
    small_spec = pl.BlockSpec((1, feat, tok), lambda s: (s, 0, 0))
    return pl.pallas_call(
        project_kernel,
        grid=(samples,),
        in_specs=[pl.BlockSpec((cols, local, width), lambda s: (0, s, 0))] + [wspec] * 4,
        out_specs=[small_spec, pl.BlockSpec((1, 2, feat, tok), lambda s: (s, 0, 0, 0)), small_spec],
        out_shape=[small, jax.ShapeDtypeStruct((samples, 2, feat, tok), BF), small],
        compiler_params=pltpu.CompilerParams(vmem_limit_bytes=VMEM),
        name="project",
    )(rows_in, wq, wk, wv, wg)


def whole_w(near, far, core):
    first = jnp.where(core == 0, near, far)
    second = jnp.where(core == 0, far, near)
    return jnp.concatenate([first, second], axis=0)


def gated_grad_kernel(core_ref, cot_ref, near_ref, far_ref, _, out_ref):
    count = cot_ref.shape[0]
    zeros = jnp.zeros((128 - 2 * HD, cot_ref.shape[1]), BF)
    for c in range(out_ref.shape[0]):
        weight = whole_w(near_ref[c], far_ref[c], core_ref[0])
        weight = jnp.concatenate([weight, zeros], axis=0)
        res = mm(cot_ref[...], weight, NT).astype(BF)
        out_ref[c, :, :128] = res[: count // 2]
        out_ref[c, :, 128:] = res[count // 2 :]


def gated_grad(core, cot, near, far, bias):
    cols, _, tok = bias.shape
    whole = lambda x: pl.BlockSpec(x.shape, lambda i: (0,) * x.ndim)
    return pl.pallas_call(
        gated_grad_kernel,
        grid=(1,),
        in_specs=[
            pl.BlockSpec(memory_space=pltpu.SMEM),
            whole(cot),
            whole(near),
            whole(far),
            pl.BlockSpec(memory_space=pl.ANY),
        ],
        out_specs=pl.BlockSpec((cols, GG_ROWS, tok), lambda i: (0, 0, 0)),
        out_shape=jax.ShapeDtypeStruct(bias.shape, BF),
        input_output_aliases={4: 0},
        compiler_params=pltpu.CompilerParams(vmem_limit_bytes=VMEM),
        name="gated_grad",
    )(core, cot, near, far, bias)


def slot_xor(t):
    return 2 * (t % 4) + t // 4


def attend_kernel(me_ref, bias_ref, q_ref, gate_ref, *refs):
    kv_refs = refs[:8]
    gated_ref, dq_ref, dgate_ref, dkv_own_ref, dkv_far_ref, dbias_ref = refs[8:14]
    s_scr, dp_scr = refs[14:]
    samples, _, tok = q_ref.shape
    head = pl.program_id(0)
    me = me_ref[0]
    scale = 1.0 / math.sqrt(HD)
    row_id = lax.broadcasted_iota(jnp.int32, (16, tok), 0)
    wanted = (row_id >= head * 3) & (row_id < head * 3 + 3)
    q = [q_ref[s] for s in range(samples)]
    sig, gg, gatt = [], [], []
    for s in range(samples):
        at = slice((s % 2) * 32, (s % 2) * 32 + 32)
        lanes = slice((s // 2) * 128, (s // 2) * 128 + 128)
        piece = bias_ref[:, at, lanes].astype(F32).reshape(tok, 128).T
        gg.append(jnp.where(head == 0, piece[:HD], piece[HD : 2 * HD]))
        sig.append(1.0 / (1.0 + jnp.exp(-gate_ref[s].astype(F32))))
        gatt.append((gg[s] * sig[s]).astype(BF))

    peak = [None] * samples
    for t in range(8):
        block = me ^ slot_xor(t)
        tops = bias_ref[block, TOP_AT:, :].astype(F32)
        top = jnp.sum(jnp.where(wanted, tops, 0.0), axis=0, keepdims=True)
        at = pl.ds(pl.multiple_of(GG_ROWS + head * 256, 64), 256)
        bias = bias_ref[block, at, :].astype(F32) + top
        for s in range(samples):
            score = mm(kv_refs[t][s, 0, :HD, :], q[s], TN) * scale + bias
            s_scr[s, t] = score
            high = jnp.max(score, axis=0, keepdims=True)
            peak[s] = high if t == 0 else jnp.maximum(peak[s], high)
    inv, dot = [], []
    for s in range(samples):
        total = jnp.zeros((1, tok), F32)
        weighted = jnp.zeros((1, tok), F32)
        for t in range(8):
            e = jnp.exp(s_scr[s, t] - peak[s])
            s_scr[s, t] = e
            dp = mm(kv_refs[t][s, 0, HD:, :], gatt[s], TN)
            dp_scr[s, t] = dp
            total = total + jnp.sum(e, axis=0, keepdims=True)
            weighted = weighted + jnp.sum(e * dp, axis=0, keepdims=True)
        inv.append(1.0 / total)
        dot.append(weighted * inv[s])
    pad = jnp.zeros((HD, tok), F32)
    pad2 = jnp.zeros((32, tok), F32)
    q_nat = [
        jnp.concatenate([q[s].astype(F32) * scale, pad, pad2], axis=0).T.astype(BF)
        for s in range(samples)
    ]
    g_nat = [
        jnp.concatenate([pad, gatt[s].astype(F32), pad2], axis=0).T.astype(BF)
        for s in range(samples)
    ]
    att = [jnp.zeros((HD, tok), F32)] * samples
    dq = [jnp.zeros((HD, tok), F32)] * samples
    for t in range(8):
        block = me ^ slot_xor(t)
        out_ref = dkv_own_ref if t < 4 else dkv_far_ref
        dbias = None
        for s in range(samples):
            prob = s_scr[s, t] * inv[s]
            prob_bf = prob.astype(BF)
            ds = prob * (dp_scr[s, t] - dot[s])
            dbias = ds if s == 0 else dbias + ds
            ds = ds.astype(BF)
            att[s] = att[s] + mm(kv_refs[t][s, 0, HD:, :], prob_bf, NN)
            dq[s] = dq[s] + mm(kv_refs[t][s, 0, :HD, :], ds, NN)
            dkv = mm(ds, q_nat[s], NN) + mm(prob_bf, g_nat[s], NN)
            out_ref[t % 4, s, 0] = dkv.T[: 2 * HD].astype(BF)
        dbias_ref[block, 0] = dbias.astype(BF)
    for s in range(samples):
        gated_ref[s] = (sig[s] * att[s]).astype(BF)
        dgate_ref[s] = (gg[s] * att[s] * sig[s] * (1.0 - sig[s])).astype(BF)
        dq_ref[s] = (dq[s] * scale).astype(BF)


def attend(me, bias, q, gate, kv):
    samples, feat, tok = q.shape
    heads = 2
    half = pl.BlockSpec((samples, HD, tok), lambda h: (0, h, 0))
    kv_spec = pl.BlockSpec((samples, 1, feat, tok), lambda h: (0, h, 0, 0))
    small = jax.ShapeDtypeStruct((samples, feat, tok), BF)
    dkv = jax.ShapeDtypeStruct((4, samples, heads, feat, tok), BF)
    dkv_spec = pl.BlockSpec((4, samples, 1, feat, tok), lambda h: (0, 0, h, 0, 0))
    return pl.pallas_call(
        attend_kernel,
        grid=(heads,),
        in_specs=[
            pl.BlockSpec(memory_space=pltpu.SMEM),
            pl.BlockSpec(bias.shape, lambda h: (0, 0, 0)),
            half,
            half,
        ]
        + [kv_spec] * 8,
        out_specs=[
            half,
            half,
            half,
            dkv_spec,
            dkv_spec,
            pl.BlockSpec((8, 1, 256, tok), lambda h: (0, h, 0, 0)),
        ],
        out_shape=[small, small, small, dkv, dkv, jax.ShapeDtypeStruct((8, heads, 256, tok), BF)],
        scratch_shapes=[pltpu.VMEM((samples, 8, 256, tok), F32)] * 2,
        compiler_params=pltpu.CompilerParams(vmem_limit_bytes=VMEM),
        cost_estimate=pl.CostEstimate(
            flops=2**34, bytes_accessed=20 * 2**20, transcendentals=2**22
        ),
        name="attend",
    )(me, bias, q, gate, *kv)


def fold_kernel(own_ref, far_ref, _, *out_refs):
    for k, out_ref in enumerate(out_refs):
        out_ref[...] = (own_ref[k].astype(F32) + far_ref[k].astype(F32)).astype(BF)


def fold(own, far, after):
    vmem = pl.BlockSpec(memory_space=pltpu.VMEM)
    return pl.pallas_call(
        fold_kernel,
        in_specs=[vmem, vmem, pl.BlockSpec(memory_space=pl.ANY)],
        out_shape=[jax.ShapeDtypeStruct(own.shape[1:], BF)] * own.shape[0],
        compiler_params=pltpu.CompilerParams(vmem_limit_bytes=VMEM),
        name="fold",
    )(own, far, after)


def norm_kernel(gated_ref, dq_ref, dg_ref, *refs):
    kv_refs = refs[:4]
    w_ref, part_ref, dcat_ref = refs[4:]
    dkv = kv_refs[0][0].astype(F32)
    for ref in kv_refs[1:]:
        dkv = dkv + ref[0].astype(F32)
    dkv = dkv.astype(BF)
    dcat = jnp.concatenate(
        [
            dq_ref[0],
            dkv[0, :HD],
            dkv[1, :HD],
            dkv[0, HD:],
            dkv[1, HD:],
            dg_ref[0],
        ],
        axis=0,
    )
    dcat_ref[0] = dcat
    cols, _, local, wide = part_ref.shape
    width = w_ref.shape[1]
    part = mm(dcat, w_ref[...], TN).astype(BF)
    part_ref[:, 0, :, :width] = part.reshape(cols, local, width)
    gated = jnp.concatenate([gated_ref[0], jnp.zeros((32, cols * local), BF)], axis=0)
    part_ref[:, 0, :, width:] = gated.astype(F32).T.astype(BF).reshape(cols, local, 128)


def norm_part(gated, dq, dg, kv_pieces, w_cat, cols):
    samples, feat, tok = dq.shape
    local = tok // cols
    all_feat, width = w_cat.shape
    half = pl.BlockSpec((1, feat, tok), lambda s: (s, 0, 0))
    kv_spec = pl.BlockSpec((1, 2, feat, tok), lambda s: (s, 0, 0, 0))
    return pl.pallas_call(
        norm_kernel,
        grid=(samples,),
        in_specs=[half, half, half]
        + [kv_spec] * 4
        + [pl.BlockSpec(w_cat.shape, lambda s: (0, 0))],
        out_specs=[
            pl.BlockSpec((cols, 1, local, width + 128), lambda s: (0, s, 0, 0)),
            pl.BlockSpec((1, all_feat, tok), lambda s: (s, 0, 0)),
        ],
        out_shape=[
            jax.ShapeDtypeStruct((cols, samples, local, width + 128), BF),
            jax.ShapeDtypeStruct((samples, all_feat, tok), BF),
        ],
        compiler_params=pltpu.CompilerParams(vmem_limit_bytes=VMEM),
        name="norm_part",
    )(gated, dq, dg, *kv_pieces, w_cat)


def weights_kernel(
    place_ref, dcat_ref, gated_ref, rows_ref, cot_ref, w_ref, gain_ref, grad_ref, gain_out_ref, acc
):
    step = pl.program_id(0)
    cols, local, width = rows_ref.shape
    dcat = dcat_ref[0]
    gated = gated_ref[0]
    grad = mm(dcat, rows_ref[...].reshape(cols * local, width), NN)
    grad_out = mm(gated, cot_ref[:, 0].reshape(cols * local, width), NN)
    four = dcat.shape[0]
    five = four + gated.shape[0]

    @pl.when(step == 0)
    def _():
        acc[:four, :] = grad
        acc[four:five, :] = grad_out
        acc[five:, :] = jnp.zeros((512 - five, width), F32)

    @pl.when(step > 0)
    def _():
        acc[:four, :] += grad
        acc[four:five, :] += grad_out

    @pl.when(step == pl.num_programs(0) - 1)
    def _():
        both = jnp.sum(acc[:four, :] * w_ref[...].astype(F32), axis=0, keepdims=True)
        gain_out_ref[...] = both / gain_ref[...]
        for p in range(8):
            grad_ref[p ^ place_ref[0]] = acc[p * 64 : (p + 1) * 64, :].astype(BF)


def weight_part(place, dcat, gated, rows_in, grad_rows, w_cat, gain):
    cols, samples, local, width = grad_rows.shape
    all_feat = w_cat.shape[0]
    feat, tok = gated.shape[1:]
    line = pl.BlockSpec((1, width), lambda s: (0, 0))
    return pl.pallas_call(
        weights_kernel,
        grid=(samples,),
        in_specs=[
            pl.BlockSpec(memory_space=pltpu.SMEM),
            pl.BlockSpec((1, all_feat, tok), lambda s: (s, 0, 0)),
            pl.BlockSpec((1, feat, tok), lambda s: (s, 0, 0)),
            pl.BlockSpec((cols, local, width), lambda s: (0, s, 0)),
            pl.BlockSpec((cols, 1, local, width), lambda s: (0, s, 0, 0)),
            pl.BlockSpec(w_cat.shape, lambda s: (0, 0)),
            line,
        ],
        out_specs=[pl.BlockSpec((8, 64, width), lambda s: (0, 0, 0)), line],
        out_shape=[
            jax.ShapeDtypeStruct((8, 64, width), BF),
            jax.ShapeDtypeStruct((1, width), F32),
        ],
        scratch_shapes=[pltpu.VMEM((512, width), F32)],
        compiler_params=pltpu.CompilerParams(vmem_limit_bytes=VMEM),
        name="weight_part",
    )(place, dcat, gated, rows_in, grad_rows, w_cat, gain)


def finish_kernel(core_ref, recv_ref, near_ref, far_ref, act_ref, cot_ref, gain_ref, out_ref, grad_ref):
    cols, samples, local, wide = recv_ref.shape
    width = act_ref.shape[-1]
    count = samples * local
    act = act_ref[...].reshape(count, width).astype(F32)
    cot = cot_ref[...].reshape(count, width).astype(F32)
    total = act
    grad_norm = jnp.zeros((count, width), F32)
    for c in range(cols):
        gated = recv_ref[c, :, :, width:].reshape(count, wide - width)[:, : 2 * HD]
        total = total + mm(gated, whole_w(near_ref[c], far_ref[c], core_ref[0]), NN)
        grad_norm = grad_norm + recv_ref[c, :, :, :width].reshape(count, width).astype(F32)
    out_ref[...] = total.astype(BF).reshape(samples, local, width)
    centred = act - jnp.mean(act, axis=-1, keepdims=True)
    inv_std = lax.rsqrt(jnp.mean(centred * centred, axis=-1, keepdims=True) + EPSILON)
    normed = centred * inv_std
    hat = grad_norm * gain_ref[...]
    back = inv_std * (
        hat
        - jnp.mean(hat, axis=-1, keepdims=True)
        - normed * jnp.mean(hat * normed, axis=-1, keepdims=True)
    )
    grad_ref[...] = (cot + back).astype(BF).reshape(samples, local, width)


def finish(core, recv, near, far, token_act, grad_out, gain):
    vmem = pl.BlockSpec(memory_space=pltpu.VMEM)
    return pl.pallas_call(
        finish_kernel,
        in_specs=[pl.BlockSpec(memory_space=pltpu.SMEM)] + [vmem] * 6,
        out_shape=[jax.ShapeDtypeStruct(token_act.shape, BF)] * 2,
        compiler_params=pltpu.CompilerParams(vmem_limit_bytes=VMEM),
        name="finish",
    )(core, recv, near, far, token_act, grad_out, gain)


def unpack_kernel(place_ref, near_ref, far_ref, *refs):
    outs, scr = refs[:5], refs[5]
    for p in range(4):
        slot = p ^ (place_ref[0] & 3)
        first = near_ref[slot].astype(F32)
        second = far_ref[slot].astype(F32)
        low = place_ref[0] < 4
        scr[p * 64 : (p + 1) * 64, :] = jnp.where(low, first, second)
        scr[256 + p * 64 : 256 + (p + 1) * 64, :] = jnp.where(low, second, first)
    feat = outs[4].shape[0]
    for k in range(5):
        outs[k][...] = scr[k * feat : (k + 1) * feat, :]


def unpack(place, near, far, feat):
    width = near.shape[-1]
    return pl.pallas_call(
        unpack_kernel,
        in_specs=[
            pl.BlockSpec(memory_space=pltpu.SMEM),
            pl.BlockSpec(memory_space=pltpu.VMEM),
            pl.BlockSpec(memory_space=pltpu.VMEM),
        ],
        out_shape=[jax.ShapeDtypeStruct((feat, width), F32)] * 5,
        scratch_shapes=[pltpu.VMEM((512, width), F32)],
        compiler_params=pltpu.CompilerParams(vmem_limit_bytes=VMEM),
        name="unpack",
    )(place, near, far)


def wpair_kernel(db_ref, pair_ref, out_ref, db_scr, acc_ref):
    step = pair_ref.shape[0]
    chans = pair_ref.shape[2]
    heads = db_scr.shape[0]

    @pl.when(pl.program_id(0) == 0)
    def _():
        acc_ref[...] = jnp.zeros_like(acc_ref)

    for h in range(heads):
        db_scr[h] = db_ref[h // 2, h % 2].astype(F32).T.astype(BF)
    for block in range(step // 16):
        left = db_scr[:, block * 16 : (block + 1) * 16, :].reshape(heads * 16, db_scr.shape[2])
        for k in range(0, 16, 2):
            pair = jnp.concatenate(
                [pair_ref[block * 16 + k], pair_ref[block * 16 + k + 1]], axis=1
            )
            at = slice(k * chans, (k + 2) * chans)
            acc_ref[:, at] += mm(left, pair, NN)

    @pl.when(pl.program_id(0) == pl.num_programs(0) - 1)
    def _():
        total = jnp.zeros((heads, chans), F32)
        row_id = lax.broadcasted_iota(jnp.int32, (heads, 16, chans), 1)
        for k in range(16):
            piece = acc_ref[:, k * chans : (k + 1) * chans].reshape(heads, 16, chans)
            total = total + jnp.sum(jnp.where(row_id == k, piece, 0.0), axis=1)
        out_ref[...] = total


def wpair_part(dbias, pair):
    groups, per, keys, rows = dbias.shape
    heads = groups * per
    chans = pair.shape[2]
    step = 128
    return pl.pallas_call(
        wpair_kernel,
        grid=(rows // step,),
        in_specs=[
            pl.BlockSpec((groups, per, keys, step), lambda i: (0, 0, 0, i)),
            pl.BlockSpec((step, keys, chans), lambda i: (i, 0, 0)),
        ],
        out_specs=pl.BlockSpec((heads, chans), lambda i: (0, 0)),
        out_shape=jax.ShapeDtypeStruct((heads, chans), F32),
        scratch_shapes=[
            pltpu.VMEM((heads, step, keys), BF),
            pltpu.VMEM((heads * 16, 16 * chans), F32),
        ],
        compiler_params=pltpu.CompilerParams(vmem_limit_bytes=VMEM),
        cost_estimate=pl.CostEstimate(flops=2**32, bytes_accessed=20 * 2**20, transcendentals=0),
        name="wpair_part",
    )(dbias, pair)


def exchange(x, axes):
    return lax.all_to_all(x, axes, 0, 0, tiled=True)


def gather(x, axes, count):
    return exchange(jnp.broadcast_to(x[None], (count,) + x.shape), axes)


def swap(x, axis, count, k):
    return lax.ppermute(x, axis, [(i, i ^ k) for i in range(count)])


def add_bf(*terms):
    total = terms[0].astype(F32)
    for term in terms[1:]:
        total = total + term.astype(F32)
    return total.astype(BF)


def add_four(x, axes):
    one, two, three = (swap(x, axes, 4, k) for k in range(1, 4))
    return (x + one) + (two + three)


def on_device(
    token_act, pair_rep, norm_gain, w_pair, w_query, w_key, w_value, w_gate, w_out, grad_out
):
    samples, local, width = token_act.shape
    feat = w_out.shape[0]
    cols = 8
    count = samples * local
    y, core, smp = (lax.axis_index(name) for name in ("y", "core", "smp"))
    me = jnp.full((1,), y * 2 + core, jnp.int32)
    which = jnp.full((1,), core, jnp.int32)
    place = jnp.full((1,), core * 4 + y, jnp.int32)

    load = prepare(which, token_act, norm_gain[None, :], w_out, cols)
    rows_in = exchange(load, COL)
    bias = pair_bias(pair_rep, w_pair)
    rows_in, bias = lax.optimization_barrier((rows_in, bias))
    w_near = rows_in[:, count:]
    w_far = swap(w_near, "core", 2, 1)
    bias = gated_grad(which, grad_out.reshape(count, width), w_near, w_far, bias)
    bias = exchange(bias, COL)

    grad_rows = gather(grad_out, COL, cols)

    wq, wk, wv, wg = w_query.T, w_key.T, w_value.T, w_gate.T
    q, kv_own, gate = project(rows_in, samples, local, wq, wk, wv, wg)
    near = [kv_own] + [swap(kv_own, "y", 4, k) for k in range(1, 4)]
    far = [swap(x, "core", 2, 1) for x in near]

    gated, dq, dgate, dkv_own, dkv_far, dbias = attend(me, bias, q, gate, near + far)
    dbias = exchange(dbias, COL)
    dkv = fold(dkv_own, swap(dkv_far, "core", 2, 1), grad_rows)
    pieces = [dkv[0]] + [swap(dkv[k], "y", 4, k) for k in range(1, 4)]
    w_cat = jnp.concatenate([wq, wk, wv, wg], axis=0)
    part, dcat = norm_part(gated, dq, dgate, pieces, w_cat, cols)
    recv = exchange(part, COL)
    blocks, gain_part = weight_part(
        place, dcat, gated, rows_in, grad_rows, w_cat, norm_gain[None, :]
    )

    blocks = add_bf(blocks[:4], swap(blocks[4:], "core", 2, 1))
    mine = add_bf(blocks[0], *(swap(blocks[k], "y", 4, k) for k in range(1, 4)))
    wpair = wpair_part(dbias, pair_rep)
    tiny = jnp.concatenate([wpair.reshape(16, 128), gain_part.reshape(6, 128)], axis=0)
    tiny = add_four(tiny, "y")
    tiny = tiny + swap(tiny, "core", 2, 1)

    tiny, mine, recv = lax.optimization_barrier((tiny, mine, recv))
    mine = add_bf(mine, swap(mine, "smp", 2, 1))
    tiny = jnp.sum(gather(tiny, COL + ("smp",), 16), axis=0)
    quad = jnp.stack([mine] + [swap(mine, "y", 4, k) for k in range(1, 4)])
    grads = unpack(place, quad, swap(quad, "core", 2, 1), feat)
    grads = [x.T for x in grads[:4]] + [grads[4]]

    block_out, grad_act = finish(
        which, recv, w_near, w_far, token_act, grad_out, norm_gain[None, :]
    )
    return (block_out, grad_act, *grads, tiny[:16].T, tiny[16:].reshape(width))


def solution(mesh):
    fine = Mesh(mesh.devices.reshape(4, 2, 4, 2, 2), ("y", "core", "z", "xh", "smp"))
    tokens = P("smp", ROW + COL, None)
    split_last = P(None, COL)
    return jax.shard_map(
        on_device,
        mesh=fine,
        in_specs=(
            tokens,
            P(ROW, COL, None),
            P(),
            P(),
            split_last,
            split_last,
            split_last,
            split_last,
            P(COL, None),
            tokens,
        ),
        out_specs=(
            tokens,
            tokens,
            split_last,
            split_last,
            split_last,
            split_last,
            P(COL, None),
            P(),
            P(),
        ),
        check_vma=False,
    )
```

```python
import functools
import math

import jax
import jax.numpy as jnp
from jax import lax
from jax.experimental import pallas as pl
from jax.experimental.pallas import tpu as pltpu
from jax.sharding import Mesh, PartitionSpec as P

EPSILON = 1e-05
BF = jnp.bfloat16
F32 = jnp.float32
HD = 48
VMEM = 56 * 2**20
COL = ("z", "xh")
ROW = ("y", "core")
GROUP = ("y", "core", "smp")

NT = (((1,), (1,)), ((), ()))
NN = (((1,), (0,)), ((), ()))
TN = (((0,), (0,)), ((), ()))


def mm(a, b, dims):
    return lax.dot_general(a, b, dims, preferred_element_type=F32)


GG_ROWS = 64
TOP_AT = GG_ROWS + 2 * 256
BIAS_ROWS = TOP_AT + 16


def bias_kernel(w_ref, pair_ref, cot_ref, out_ref, cot_out_ref, acc_ref):
    heads, rows, keys = acc_ref.shape
    for c in range(cot_out_ref.shape[0]):
        cot_out_ref[c] = cot_ref[...]
    for block in range(rows // 16):
        piece = jnp.concatenate([pair_ref[block * 16 + k] for k in range(16)], axis=1)
        res = mm(w_ref[...], piece, NT)
        acc_ref[:, block * 16 : (block + 1) * 16, :] = res.reshape(heads, 16, keys)
    row_id = lax.broadcasted_iota(jnp.int32, (16, rows), 0)
    for group in range(heads // 2):
        tops = jnp.zeros((16, rows), F32)
        for half in range(2):
            tile = acc_ref[group * 2 + half].T
            top = jnp.max(tile, axis=0, keepdims=True)
            at = GG_ROWS + half * keys
            out_ref[group, at : at + keys, :] = (tile - top).astype(BF)
            one = top.astype(BF).astype(F32)
            two = (top - one).astype(BF).astype(F32)
            for k, term in enumerate((one, two, top - one - two)):
                tops = jnp.where(row_id == half * 3 + k, term, tops)
        out_ref[group, TOP_AT:, :] = tops.astype(BF)


def pair_bias(pair, w_pair, cot):
    rows, keys, chans = pair.shape
    heads = w_pair.shape[1]
    eye = jnp.eye(16, dtype=BF)
    spread = (w_pair.T[:, None, None, :] * eye[None, :, :, None]).reshape(heads * 16, 16 * chans)
    step = 128
    return pl.pallas_call(
        bias_kernel,
        grid=(rows // step,),
        in_specs=[
            pl.BlockSpec(spread.shape, lambda i: (0, 0)),
            pl.BlockSpec((step, keys, chans), lambda i: (i, 0, 0)),
            pl.BlockSpec(cot.shape, lambda i: (0, 0, 0)),
        ],
        out_specs=[
            pl.BlockSpec((heads // 2, BIAS_ROWS, step), lambda i: (0, 0, i)),
            pl.BlockSpec((heads * step // 2 // rows,) + cot.shape, lambda i: (i, 0, 0, 0)),
        ],
        out_shape=[
            jax.ShapeDtypeStruct((heads // 2, BIAS_ROWS, rows), BF),
            jax.ShapeDtypeStruct((heads // 2,) + cot.shape, BF),
        ],
        scratch_shapes=[pltpu.VMEM((heads, step, keys), F32)],
        compiler_params=pltpu.CompilerParams(vmem_limit_bytes=VMEM),
        cost_estimate=pl.CostEstimate(flops=2**34, bytes_accessed=2**25, transcendentals=0),
        name="pair_bias",
    )(spread, pair, cot)


def prepare_kernel(core_ref, act_ref, gain_ref, w_ref, out_ref):
    samples, local, width = act_ref.shape
    act = act_ref[...].reshape(samples * local, width).astype(F32)
    centred = act - jnp.mean(act, axis=-1, keepdims=True)
    inv_std = lax.rsqrt(jnp.mean(centred * centred, axis=-1, keepdims=True) + EPSILON)
    gain = gain_ref[...].reshape(1, width)
    norm = (centred * inv_std * gain).astype(BF)
    half = w_ref[pl.ds(pl.multiple_of(core_ref[0] * HD, 16), HD), :]
    for c in range(out_ref.shape[0]):
        out_ref[c, : samples * local, :] = norm
        out_ref[c, samples * local :, :] = half


def prepare(core, token_act, gain, w_out, cols):
    samples, local, width = token_act.shape
    vmem = pl.BlockSpec(memory_space=pltpu.VMEM)
    return pl.pallas_call(
        prepare_kernel,
        in_specs=[pl.BlockSpec(memory_space=pltpu.SMEM), vmem, vmem, vmem],
        out_shape=jax.ShapeDtypeStruct((cols, samples * local + HD, width), BF),
        compiler_params=pltpu.CompilerParams(vmem_limit_bytes=VMEM),
        name="prepare",
    )(core, token_act, gain, w_out)


def project_kernel(rows_ref, wq_ref, wk_ref, wv_ref, wg_ref, q_ref, kv_ref, g_ref):
    rows = rows_ref[...].reshape(256, rows_ref.shape[-1])
    q_ref[0] = mm(wq_ref[...], rows, NT).astype(BF)
    g_ref[0] = mm(wg_ref[...], rows, NT).astype(BF)
    keys = mm(wk_ref[...], rows, NT).astype(BF)
    values = mm(wv_ref[...], rows, NT).astype(BF)
    for h in range(2):
        kv_ref[0, h, :HD, :] = keys[h * HD : (h + 1) * HD, :]
        kv_ref[0, h, HD:, :] = values[h * HD : (h + 1) * HD, :]


def project(rows_in, samples, local, wq, wk, wv, wg):
    cols, _, width = rows_in.shape
    feat = wq.shape[0]
    tok = cols * local
    wspec = pl.BlockSpec((feat, width), lambda s: (0, 0))
    small = jax.ShapeDtypeStruct((samples, feat, tok), BF)
    small_spec = pl.BlockSpec((1, feat, tok), lambda s: (s, 0, 0))
    return pl.pallas_call(
        project_kernel,
        grid=(samples,),
        in_specs=[pl.BlockSpec((cols, local, width), lambda s: (0, s, 0))] + [wspec] * 4,
        out_specs=[small_spec, pl.BlockSpec((1, 2, feat, tok), lambda s: (s, 0, 0, 0)), small_spec],
        out_shape=[small, jax.ShapeDtypeStruct((samples, 2, feat, tok), BF), small],
        compiler_params=pltpu.CompilerParams(vmem_limit_bytes=VMEM),
        name="project",
    )(rows_in, wq, wk, wv, wg)


def whole_w(near, far, core):
    first = jnp.where(core == 0, near, far)
    second = jnp.where(core == 0, far, near)
    return jnp.concatenate([first, second], axis=0)


def gated_grad_kernel(core_ref, cot_ref, near_ref, far_ref, _, out_ref):
    count = cot_ref.shape[0]
    zeros = jnp.zeros((128 - 2 * HD, cot_ref.shape[1]), BF)
    for c in range(out_ref.shape[0]):
        weight = whole_w(near_ref[c], far_ref[c], core_ref[0])
        weight = jnp.concatenate([weight, zeros], axis=0)
        res = mm(cot_ref[...], weight, NT).astype(BF)
        out_ref[c, :, :128] = res[: count // 2]
        out_ref[c, :, 128:] = res[count // 2 :]


def gated_grad(core, cot, near, far, bias):
    cols, _, tok = bias.shape
    whole = lambda x: pl.BlockSpec(x.shape, lambda i: (0,) * x.ndim)
    return pl.pallas_call(
        gated_grad_kernel,
        grid=(1,),
        in_specs=[
            pl.BlockSpec(memory_space=pltpu.SMEM),
            whole(cot),
            whole(near),
            whole(far),
            pl.BlockSpec(memory_space=pl.ANY),
        ],
        out_specs=pl.BlockSpec((cols, GG_ROWS, tok), lambda i: (0, 0, 0)),
        out_shape=jax.ShapeDtypeStruct(bias.shape, BF),
        input_output_aliases={4: 0},
        compiler_params=pltpu.CompilerParams(vmem_limit_bytes=VMEM),
        name="gated_grad",
    )(core, cot, near, far, bias)


def slot_xor(t):
    return 2 * (t % 4) + t // 4


def attend_kernel(me_ref, bias_ref, q_ref, gate_ref, *refs):
    kv_refs = refs[:8]
    gated_ref, dq_ref, dgate_ref, dkv_own_ref, dkv_far_ref, dbias_ref = refs[8:14]
    s_scr, dp_scr = refs[14:]
    samples, _, tok = q_ref.shape
    head = pl.program_id(0)
    me = me_ref[0]
    scale = 1.0 / math.sqrt(HD)
    row_id = lax.broadcasted_iota(jnp.int32, (16, tok), 0)
    wanted = (row_id >= head * 3) & (row_id < head * 3 + 3)
    q = [q_ref[s] for s in range(samples)]
    sig, gg, gatt = [], [], []
    for s in range(samples):
        at = slice((s % 2) * 32, (s % 2) * 32 + 32)
        lanes = slice((s // 2) * 128, (s // 2) * 128 + 128)
        piece = bias_ref[:, at, lanes].astype(F32).reshape(tok, 128).T
        gg.append(jnp.where(head == 0, piece[:HD], piece[HD : 2 * HD]))
        sig.append(1.0 / (1.0 + jnp.exp(-gate_ref[s].astype(F32))))
        gatt.append((gg[s] * sig[s]).astype(BF))

    peak = [None] * samples
    for t in range(8):
        block = me ^ slot_xor(t)
        tops = bias_ref[block, TOP_AT:, :].astype(F32)
        top = jnp.sum(jnp.where(wanted, tops, 0.0), axis=0, keepdims=True)
        at = pl.ds(pl.multiple_of(GG_ROWS + head * 256, 64), 256)
        bias = bias_ref[block, at, :].astype(F32) + top
        for s in range(samples):
            score = mm(kv_refs[t][s, 0, :HD, :], q[s], TN) * scale + bias
            s_scr[s, t] = score
            high = jnp.max(score, axis=0, keepdims=True)
            peak[s] = high if t == 0 else jnp.maximum(peak[s], high)
    inv, dot = [], []
    for s in range(samples):
        total = jnp.zeros((1, tok), F32)
        weighted = jnp.zeros((1, tok), F32)
        for t in range(8):
            e = jnp.exp(s_scr[s, t] - peak[s])
            s_scr[s, t] = e
            dp = mm(kv_refs[t][s, 0, HD:, :], gatt[s], TN)
            dp_scr[s, t] = dp
            total = total + jnp.sum(e, axis=0, keepdims=True)
            weighted = weighted + jnp.sum(e * dp, axis=0, keepdims=True)
        inv.append(1.0 / total)
        dot.append(weighted * inv[s])
    pad = jnp.zeros((HD, tok), F32)
    pad2 = jnp.zeros((32, tok), F32)
    q_nat = [
        jnp.concatenate([q[s].astype(F32) * scale, pad, pad2], axis=0).T.astype(BF)
        for s in range(samples)
    ]
    g_nat = [
        jnp.concatenate([pad, gatt[s].astype(F32), pad2], axis=0).T.astype(BF)
        for s in range(samples)
    ]
    att = [jnp.zeros((HD, tok), F32)] * samples
    dq = [jnp.zeros((HD, tok), F32)] * samples
    for t in range(8):
        block = me ^ slot_xor(t)
        out_ref = dkv_own_ref if t < 4 else dkv_far_ref
        dbias = None
        for s in range(samples):
            prob = s_scr[s, t] * inv[s]
            prob_bf = prob.astype(BF)
            ds = prob * (dp_scr[s, t] - dot[s])
            dbias = ds if s == 0 else dbias + ds
            ds = ds.astype(BF)
            att[s] = att[s] + mm(kv_refs[t][s, 0, HD:, :], prob_bf, NN)
            dq[s] = dq[s] + mm(kv_refs[t][s, 0, :HD, :], ds, NN)
            dkv = mm(ds, q_nat[s], NN) + mm(prob_bf, g_nat[s], NN)
            out_ref[t % 4, s, 0] = dkv.T[: 2 * HD].astype(BF)
        dbias_ref[block, 0] = dbias.astype(BF)
    for s in range(samples):
        gated_ref[s] = (sig[s] * att[s]).astype(BF)
        dgate_ref[s] = (gg[s] * att[s] * sig[s] * (1.0 - sig[s])).astype(BF)
        dq_ref[s] = (dq[s] * scale).astype(BF)


def attend(me, bias, q, gate, kv):
    samples, feat, tok = q.shape
    heads = 2
    half = pl.BlockSpec((samples, HD, tok), lambda h: (0, h, 0))
    kv_spec = pl.BlockSpec((samples, 1, feat, tok), lambda h: (0, h, 0, 0))
    small = jax.ShapeDtypeStruct((samples, feat, tok), BF)
    dkv = jax.ShapeDtypeStruct((4, samples, heads, feat, tok), BF)
    dkv_spec = pl.BlockSpec((4, samples, 1, feat, tok), lambda h: (0, 0, h, 0, 0))
    return pl.pallas_call(
        attend_kernel,
        grid=(heads,),
        in_specs=[
            pl.BlockSpec(memory_space=pltpu.SMEM),
            pl.BlockSpec(bias.shape, lambda h: (0, 0, 0)),
            half,
            half,
        ]
        + [kv_spec] * 8,
        out_specs=[
            half,
            half,
            half,
            dkv_spec,
            dkv_spec,
            pl.BlockSpec((8, 1, 256, tok), lambda h: (0, h, 0, 0)),
        ],
        out_shape=[small, small, small, dkv, dkv, jax.ShapeDtypeStruct((8, heads, 256, tok), BF)],
        scratch_shapes=[pltpu.VMEM((samples, 8, 256, tok), F32)] * 2,
        compiler_params=pltpu.CompilerParams(vmem_limit_bytes=VMEM),
        cost_estimate=pl.CostEstimate(
            flops=2**34, bytes_accessed=20 * 2**20, transcendentals=2**22
        ),
        name="attend",
    )(me, bias, q, gate, *kv)


def fold_kernel(own_ref, far_ref, _, *out_refs):
    for k, out_ref in enumerate(out_refs):
        out_ref[...] = (own_ref[k].astype(F32) + far_ref[k].astype(F32)).astype(BF)


def fold(own, far, after):
    vmem = pl.BlockSpec(memory_space=pltpu.VMEM)
    return pl.pallas_call(
        fold_kernel,
        in_specs=[vmem, vmem, pl.BlockSpec(memory_space=pl.ANY)],
        out_shape=[jax.ShapeDtypeStruct(own.shape[1:], BF)] * own.shape[0],
        compiler_params=pltpu.CompilerParams(vmem_limit_bytes=VMEM),
        name="fold",
    )(own, far, after)


def norm_kernel(gated_ref, dq_ref, dg_ref, *refs):
    kv_refs = refs[:4]
    w_ref, part_ref, dcat_ref = refs[4:]
    dkv = kv_refs[0][0].astype(F32)
    for ref in kv_refs[1:]:
        dkv = dkv + ref[0].astype(F32)
    dkv = dkv.astype(BF)
    dcat = jnp.concatenate(
        [
            dq_ref[0],
            dkv[0, :HD],
            dkv[1, :HD],
            dkv[0, HD:],
            dkv[1, HD:],
            dg_ref[0],
        ],
        axis=0,
    )
    dcat_ref[0] = dcat
    cols, _, local, wide = part_ref.shape
    width = w_ref.shape[1]
    part = mm(dcat, w_ref[...], TN).astype(BF)
    part_ref[:, 0, :, :width] = part.reshape(cols, local, width)
    gated = jnp.concatenate([gated_ref[0], jnp.zeros((32, cols * local), BF)], axis=0)
    part_ref[:, 0, :, width:] = gated.astype(F32).T.astype(BF).reshape(cols, local, 128)


def norm_part(gated, dq, dg, kv_pieces, w_cat, cols):
    samples, feat, tok = dq.shape
    local = tok // cols
    all_feat, width = w_cat.shape
    half = pl.BlockSpec((1, feat, tok), lambda s: (s, 0, 0))
    kv_spec = pl.BlockSpec((1, 2, feat, tok), lambda s: (s, 0, 0, 0))
    return pl.pallas_call(
        norm_kernel,
        grid=(samples,),
        in_specs=[half, half, half]
        + [kv_spec] * 4
        + [pl.BlockSpec(w_cat.shape, lambda s: (0, 0))],
        out_specs=[
            pl.BlockSpec((cols, 1, local, width + 128), lambda s: (0, s, 0, 0)),
            pl.BlockSpec((1, all_feat, tok), lambda s: (s, 0, 0)),
        ],
        out_shape=[
            jax.ShapeDtypeStruct((cols, samples, local, width + 128), BF),
            jax.ShapeDtypeStruct((samples, all_feat, tok), BF),
        ],
        compiler_params=pltpu.CompilerParams(vmem_limit_bytes=VMEM),
        name="norm_part",
    )(gated, dq, dg, *kv_pieces, w_cat)


def weights_kernel(
    place_ref, dcat_ref, gated_ref, rows_ref, cot_ref, w_ref, gain_ref, grad_ref, gain_out_ref, acc
):
    step = pl.program_id(0)
    cols, local, width = rows_ref.shape
    dcat = dcat_ref[0]
    gated = gated_ref[0]
    grad = mm(dcat, rows_ref[...].reshape(cols * local, width), NN)
    grad_out = mm(gated, cot_ref[:, 0].reshape(cols * local, width), NN)
    four = dcat.shape[0]
    five = four + gated.shape[0]

    @pl.when(step == 0)
    def _():
        acc[:four, :] = grad
        acc[four:five, :] = grad_out
        acc[five:, :] = jnp.zeros((512 - five, width), F32)

    @pl.when(step > 0)
    def _():
        acc[:four, :] += grad
        acc[four:five, :] += grad_out

    @pl.when(step == pl.num_programs(0) - 1)
    def _():
        both = jnp.sum(acc[:four, :] * w_ref[...].astype(F32), axis=0, keepdims=True)
        gain_out_ref[...] = both / gain_ref[...]
        for p in range(8):
            grad_ref[p ^ place_ref[0]] = acc[p * 64 : (p + 1) * 64, :].astype(BF)


def weight_part(place, dcat, gated, rows_in, grad_rows, w_cat, gain):
    cols, samples, local, width = grad_rows.shape
    all_feat = w_cat.shape[0]
    feat, tok = gated.shape[1:]
    line = pl.BlockSpec((1, width), lambda s: (0, 0))
    return pl.pallas_call(
        weights_kernel,
        grid=(samples,),
        in_specs=[
            pl.BlockSpec(memory_space=pltpu.SMEM),
            pl.BlockSpec((1, all_feat, tok), lambda s: (s, 0, 0)),
            pl.BlockSpec((1, feat, tok), lambda s: (s, 0, 0)),
            pl.BlockSpec((cols, local, width), lambda s: (0, s, 0)),
            pl.BlockSpec((cols, 1, local, width), lambda s: (0, s, 0, 0)),
            pl.BlockSpec(w_cat.shape, lambda s: (0, 0)),
            line,
        ],
        out_specs=[pl.BlockSpec((8, 64, width), lambda s: (0, 0, 0)), line],
        out_shape=[
            jax.ShapeDtypeStruct((8, 64, width), BF),
            jax.ShapeDtypeStruct((1, width), F32),
        ],
        scratch_shapes=[pltpu.VMEM((512, width), F32)],
        compiler_params=pltpu.CompilerParams(vmem_limit_bytes=VMEM),
        name="weight_part",
    )(place, dcat, gated, rows_in, grad_rows, w_cat, gain)


def finish_kernel(core_ref, recv_ref, near_ref, far_ref, act_ref, cot_ref, gain_ref, out_ref, grad_ref):
    cols, samples, local, wide = recv_ref.shape
    width = act_ref.shape[-1]
    count = samples * local
    act = act_ref[...].reshape(count, width).astype(F32)
    cot = cot_ref[...].reshape(count, width).astype(F32)
    total = act
    grad_norm = jnp.zeros((count, width), F32)
    for c in range(cols):
        gated = recv_ref[c, :, :, width:].reshape(count, wide - width)[:, : 2 * HD]
        total = total + mm(gated, whole_w(near_ref[c], far_ref[c], core_ref[0]), NN)
        grad_norm = grad_norm + recv_ref[c, :, :, :width].reshape(count, width).astype(F32)
    out_ref[...] = total.astype(BF).reshape(samples, local, width)
    centred = act - jnp.mean(act, axis=-1, keepdims=True)
    inv_std = lax.rsqrt(jnp.mean(centred * centred, axis=-1, keepdims=True) + EPSILON)
    normed = centred * inv_std
    hat = grad_norm * gain_ref[...]
    back = inv_std * (
        hat
        - jnp.mean(hat, axis=-1, keepdims=True)
        - normed * jnp.mean(hat * normed, axis=-1, keepdims=True)
    )
    grad_ref[...] = (cot + back).astype(BF).reshape(samples, local, width)


def finish(core, recv, near, far, token_act, grad_out, gain):
    vmem = pl.BlockSpec(memory_space=pltpu.VMEM)
    return pl.pallas_call(
        finish_kernel,
        in_specs=[pl.BlockSpec(memory_space=pltpu.SMEM)] + [vmem] * 6,
        out_shape=[jax.ShapeDtypeStruct(token_act.shape, BF)] * 2,
        compiler_params=pltpu.CompilerParams(vmem_limit_bytes=VMEM),
        name="finish",
    )(core, recv, near, far, token_act, grad_out, gain)


def unpack_kernel(place_ref, near_ref, far_ref, *refs):
    outs, scr = refs[:5], refs[5]
    for p in range(4):
        slot = p ^ (place_ref[0] & 3)
        first = near_ref[slot].astype(F32)
        second = far_ref[slot].astype(F32)
        low = place_ref[0] < 4
        scr[p * 64 : (p + 1) * 64, :] = jnp.where(low, first, second)
        scr[256 + p * 64 : 256 + (p + 1) * 64, :] = jnp.where(low, second, first)
    feat = outs[4].shape[0]
    for k in range(5):
        outs[k][...] = scr[k * feat : (k + 1) * feat, :]


def unpack(place, near, far, feat):
    width = near.shape[-1]
    return pl.pallas_call(
        unpack_kernel,
        in_specs=[
            pl.BlockSpec(memory_space=pltpu.SMEM),
            pl.BlockSpec(memory_space=pltpu.VMEM),
            pl.BlockSpec(memory_space=pltpu.VMEM),
        ],
        out_shape=[jax.ShapeDtypeStruct((feat, width), F32)] * 5,
        scratch_shapes=[pltpu.VMEM((512, width), F32)],
        compiler_params=pltpu.CompilerParams(vmem_limit_bytes=VMEM),
        name="unpack",
    )(place, near, far)


def wpair_kernel(db_ref, pair_ref, out_ref, db_scr, acc_ref):
    step = pair_ref.shape[0]
    chans = pair_ref.shape[2]
    heads = db_scr.shape[0]

    @pl.when(pl.program_id(0) == 0)
    def _():
        acc_ref[...] = jnp.zeros_like(acc_ref)

    for h in range(heads):
        db_scr[h] = db_ref[h // 2, h % 2].astype(F32).T.astype(BF)
    for block in range(step // 16):
        left = db_scr[:, block * 16 : (block + 1) * 16, :].reshape(heads * 16, db_scr.shape[2])
        for k in range(0, 16, 2):
            pair = jnp.concatenate(
                [pair_ref[block * 16 + k], pair_ref[block * 16 + k + 1]], axis=1
            )
            at = slice(k * chans, (k + 2) * chans)
            acc_ref[:, at] += mm(left, pair, NN)

    @pl.when(pl.program_id(0) == pl.num_programs(0) - 1)
    def _():
        total = jnp.zeros((heads, chans), F32)
        row_id = lax.broadcasted_iota(jnp.int32, (heads, 16, chans), 1)
        for k in range(16):
            piece = acc_ref[:, k * chans : (k + 1) * chans].reshape(heads, 16, chans)
            total = total + jnp.sum(jnp.where(row_id == k, piece, 0.0), axis=1)
        out_ref[...] = total


def wpair_part(dbias, pair):
    groups, per, keys, rows = dbias.shape
    heads = groups * per
    chans = pair.shape[2]
    step = 128
    return pl.pallas_call(
        wpair_kernel,
        grid=(rows // step,),
        in_specs=[
            pl.BlockSpec((groups, per, keys, step), lambda i: (0, 0, 0, i)),
            pl.BlockSpec((step, keys, chans), lambda i: (i, 0, 0)),
        ],
        out_specs=pl.BlockSpec((heads, chans), lambda i: (0, 0)),
        out_shape=jax.ShapeDtypeStruct((heads, chans), F32),
        scratch_shapes=[
            pltpu.VMEM((heads, step, keys), BF),
            pltpu.VMEM((heads * 16, 16 * chans), F32),
        ],
        compiler_params=pltpu.CompilerParams(vmem_limit_bytes=VMEM),
        cost_estimate=pl.CostEstimate(flops=2**32, bytes_accessed=20 * 2**20, transcendentals=0),
        name="wpair_part",
    )(dbias, pair)


def exchange(x, axes):
    return lax.all_to_all(x, axes, 0, 0, tiled=True)


def gather(x, axes, count):
    return exchange(jnp.broadcast_to(x[None], (count,) + x.shape), axes)


def swap(x, axis, count, k):
    return lax.ppermute(x, axis, [(i, i ^ k) for i in range(count)])


def add_bf(*terms):
    total = terms[0].astype(F32)
    for term in terms[1:]:
        total = total + term.astype(F32)
    return total.astype(BF)


def add_four(x, axes):
    one, two, three = (swap(x, axes, 4, k) for k in range(1, 4))
    return (x + one) + (two + three)


def on_device(
    token_act, pair_rep, norm_gain, w_pair, w_query, w_key, w_value, w_gate, w_out, grad_out
):
    samples, local, width = token_act.shape
    feat = w_out.shape[0]
    cols = 8
    count = samples * local
    y, core, smp = (lax.axis_index(name) for name in ("y", "core", "smp"))
    me = jnp.full((1,), y * 2 + core, jnp.int32)
    which = jnp.full((1,), core, jnp.int32)
    place = jnp.full((1,), core * 4 + y, jnp.int32)

    load = prepare(which, token_act, norm_gain, w_out, cols)
    rows_in = exchange(load, COL)
    bias, cot_load = pair_bias(pair_rep, w_pair, grad_out)
    rows_in, bias = lax.optimization_barrier((rows_in, bias))
    w_near = rows_in[:, count:]
    w_far = swap(w_near, "core", 2, 1)
    bias = gated_grad(which, grad_out.reshape(count, width), w_near, w_far, bias)
    bias = exchange(bias, COL)

    grad_rows = exchange(cot_load, COL)

    wq, wk, wv, wg = w_query.T, w_key.T, w_value.T, w_gate.T
    q, kv_own, gate = project(rows_in, samples, local, wq, wk, wv, wg)
    near = [kv_own] + [swap(kv_own, "y", 4, k) for k in range(1, 4)]
    far = [swap(x, "core", 2, 1) for x in near]

    gated, dq, dgate, dkv_own, dkv_far, dbias = attend(me, bias, q, gate, near + far)
    dbias = exchange(dbias, COL)
    dkv = fold(dkv_own, swap(dkv_far, "core", 2, 1), grad_rows)
    pieces = [dkv[0]] + [swap(dkv[k], "y", 4, k) for k in range(1, 4)]
    w_cat = jnp.concatenate([wq, wk, wv, wg], axis=0)
    part, dcat = norm_part(gated, dq, dgate, pieces, w_cat, cols)
    recv = exchange(part, COL)
    blocks, gain_part = weight_part(
        place, dcat, gated, rows_in, grad_rows, w_cat, norm_gain[None, :]
    )

    blocks = add_bf(blocks[:4], swap(blocks[4:], "core", 2, 1))
    mine = add_bf(blocks[0], *(swap(blocks[k], "y", 4, k) for k in range(1, 4)))
    wpair = wpair_part(dbias, pair_rep)
    tiny = jnp.concatenate([wpair.reshape(16, 128), gain_part.reshape(6, 128)], axis=0)
    tiny = add_four(tiny, "y")
    tiny = tiny + swap(tiny, "core", 2, 1)

    tiny, mine, recv = lax.optimization_barrier((tiny, mine, recv))
    mine = add_bf(mine, swap(mine, "smp", 2, 1))
    tiny = jnp.sum(gather(tiny, COL + ("smp",), 16), axis=0)
    quad = jnp.stack([mine] + [swap(mine, "y", 4, k) for k in range(1, 4)])
    grads = unpack(place, quad, swap(quad, "core", 2, 1), feat)
    grads = [x.T for x in grads[:4]] + [grads[4]]

    block_out, grad_act = finish(
        which, recv, w_near, w_far, token_act, grad_out, norm_gain[None, :]
    )
    return (block_out, grad_act, *grads, tiny[:16].T, tiny[16:].reshape(width))


def solution(mesh):
    fine = Mesh(mesh.devices.reshape(4, 2, 4, 2, 2), ("y", "core", "z", "xh", "smp"))
    tokens = P("smp", ROW + COL, None)
    split_last = P(None, COL)
    return jax.shard_map(
        on_device,
        mesh=fine,
        in_specs=(
            tokens,
            P(ROW, COL, None),
            P(),
            P(),
            split_last,
            split_last,
            split_last,
            split_last,
            P(COL, None),
            tokens,
        ),
        out_specs=(
            tokens,
            tokens,
            split_last,
            split_last,
            split_last,
            split_last,
            P(COL, None),
            P(),
            P(),
        ),
        check_vma=False,
    )
```

```python
import functools
import math

import jax
import jax.numpy as jnp
from jax import lax
from jax.experimental import pallas as pl
from jax.experimental.pallas import tpu as pltpu
from jax.sharding import Mesh, PartitionSpec as P

EPSILON = 1e-05
BF = jnp.bfloat16
F32 = jnp.float32
HD = 48
VMEM = 56 * 2**20
COL = ("z", "xh")
ROW = ("y", "core")
GROUP = ("y", "core", "smp")

NT = (((1,), (1,)), ((), ()))
NN = (((1,), (0,)), ((), ()))
TN = (((0,), (0,)), ((), ()))


def mm(a, b, dims):
    return lax.dot_general(a, b, dims, preferred_element_type=F32)


GG_ROWS = 64
TOP_AT = GG_ROWS + 2 * 256
BIAS_ROWS = TOP_AT + 16


def bias_kernel(w_ref, pair_ref, cot_ref, out_ref, cot_out_ref, acc_ref):
    heads, rows, keys = acc_ref.shape
    for c in range(cot_out_ref.shape[0]):
        cot_out_ref[c] = cot_ref[...]
    for block in range(rows // 16):
        piece = jnp.concatenate([pair_ref[block * 16 + k] for k in range(16)], axis=1)
        res = mm(w_ref[...], piece, NT)
        acc_ref[:, block * 16 : (block + 1) * 16, :] = res.reshape(heads, 16, keys)
    row_id = lax.broadcasted_iota(jnp.int32, (16, rows), 0)
    for group in range(heads // 2):
        tops = jnp.zeros((16, rows), F32)
        for half in range(2):
            tile = acc_ref[group * 2 + half].T
            top = jnp.max(tile, axis=0, keepdims=True)
            at = GG_ROWS + half * keys
            out_ref[group, at : at + keys, :] = (tile - top).astype(BF)
            one = top.astype(BF).astype(F32)
            two = (top - one).astype(BF).astype(F32)
            for k, term in enumerate((one, two, top - one - two)):
                tops = jnp.where(row_id == half * 3 + k, term, tops)
        out_ref[group, TOP_AT:, :] = tops.astype(BF)


def pair_bias(pair, w_pair, cot):
    rows, keys, chans = pair.shape
    heads = w_pair.shape[1]
    eye = jnp.eye(16, dtype=BF)
    spread = (w_pair.T[:, None, None, :] * eye[None, :, :, None]).reshape(heads * 16, 16 * chans)
    step = 128
    return pl.pallas_call(
        bias_kernel,
        grid=(rows // step,),
        in_specs=[
            pl.BlockSpec(spread.shape, lambda i: (0, 0)),
            pl.BlockSpec((step, keys, chans), lambda i: (i, 0, 0)),
            pl.BlockSpec(cot.shape, lambda i: (0, 0, 0)),
        ],
        out_specs=[
            pl.BlockSpec((heads // 2, BIAS_ROWS, step), lambda i: (0, 0, i)),
            pl.BlockSpec((heads * step // 2 // rows,) + cot.shape, lambda i: (i, 0, 0, 0)),
        ],
        out_shape=[
            jax.ShapeDtypeStruct((heads // 2, BIAS_ROWS, rows), BF),
            jax.ShapeDtypeStruct((heads // 2,) + cot.shape, BF),
        ],
        scratch_shapes=[pltpu.VMEM((heads, step, keys), F32)],
        compiler_params=pltpu.CompilerParams(vmem_limit_bytes=VMEM),
        cost_estimate=pl.CostEstimate(flops=2**34, bytes_accessed=2**25, transcendentals=0),
        name="pair_bias",
    )(spread, pair, cot)


def prepare_kernel(core_ref, act_ref, gain_ref, w_ref, out_ref):
    samples, local, width = act_ref.shape
    act = act_ref[...].reshape(samples * local, width).astype(F32)
    centred = act - jnp.mean(act, axis=-1, keepdims=True)
    inv_std = lax.rsqrt(jnp.mean(centred * centred, axis=-1, keepdims=True) + EPSILON)
    gain = gain_ref[...].reshape(1, width)
    norm = (centred * inv_std * gain).astype(BF)
    half = w_ref[pl.ds(pl.multiple_of(core_ref[0] * HD, 16), HD), :]
    for c in range(out_ref.shape[0]):
        out_ref[c, : samples * local, :] = norm
        out_ref[c, samples * local :, :] = half


def prepare(core, token_act, gain, w_out, cols):
    samples, local, width = token_act.shape
    vmem = pl.BlockSpec(memory_space=pltpu.VMEM)
    return pl.pallas_call(
        prepare_kernel,
        in_specs=[pl.BlockSpec(memory_space=pltpu.SMEM), vmem, vmem, vmem],
        out_shape=jax.ShapeDtypeStruct((cols, samples * local + HD, width), BF),
        compiler_params=pltpu.CompilerParams(vmem_limit_bytes=VMEM),
        name="prepare",
    )(core, token_act, gain, w_out)


def project_kernel(rows_ref, wq_ref, wk_ref, wv_ref, wg_ref, q_ref, kv_ref, g_ref):
    rows = rows_ref[...].reshape(256, rows_ref.shape[-1])
    q_ref[0] = mm(wq_ref[...], rows, NT).astype(BF)
    g_ref[0] = mm(wg_ref[...], rows, NT).astype(BF)
    keys = mm(wk_ref[...], rows, NT).astype(BF)
    values = mm(wv_ref[...], rows, NT).astype(BF)
    for h in range(2):
        kv_ref[0, h, :HD, :] = keys[h * HD : (h + 1) * HD, :]
        kv_ref[0, h, HD:, :] = values[h * HD : (h + 1) * HD, :]


def project(rows_in, samples, local, wq, wk, wv, wg):
    cols, _, width = rows_in.shape
    feat = wq.shape[0]
    tok = cols * local
    wspec = pl.BlockSpec((feat, width), lambda s: (0, 0))
    small = jax.ShapeDtypeStruct((samples, feat, tok), BF)
    small_spec = pl.BlockSpec((1, feat, tok), lambda s: (s, 0, 0))
    return pl.pallas_call(
        project_kernel,
        grid=(samples,),
        in_specs=[pl.BlockSpec((cols, local, width), lambda s: (0, s, 0))] + [wspec] * 4,
        out_specs=[small_spec, pl.BlockSpec((1, 2, feat, tok), lambda s: (s, 0, 0, 0)), small_spec],
        out_shape=[small, jax.ShapeDtypeStruct((samples, 2, feat, tok), BF), small],
        compiler_params=pltpu.CompilerParams(vmem_limit_bytes=VMEM),
        name="project",
    )(rows_in, wq, wk, wv, wg)


def whole_w(near, far, core):
    first = jnp.where(core == 0, near, far)
    second = jnp.where(core == 0, far, near)
    return jnp.concatenate([first, second], axis=0)


def gated_grad_kernel(core_ref, cot_ref, near_ref, far_ref, _, out_ref):
    count = cot_ref.shape[0]
    zeros = jnp.zeros((128 - 2 * HD, cot_ref.shape[1]), BF)
    for c in range(out_ref.shape[0]):
        weight = whole_w(near_ref[c], far_ref[c], core_ref[0])
        weight = jnp.concatenate([weight, zeros], axis=0)
        res = mm(cot_ref[...], weight, NT).astype(BF)
        out_ref[c, :, :128] = res[: count // 2]
        out_ref[c, :, 128:] = res[count // 2 :]


def gated_grad(core, cot, near, far, bias):
    cols, _, tok = bias.shape
    whole = lambda x: pl.BlockSpec(x.shape, lambda i: (0,) * x.ndim)
    return pl.pallas_call(
        gated_grad_kernel,
        grid=(1,),
        in_specs=[
            pl.BlockSpec(memory_space=pltpu.SMEM),
            whole(cot),
            whole(near),
            whole(far),
            pl.BlockSpec(memory_space=pl.ANY),
        ],
        out_specs=pl.BlockSpec((cols, GG_ROWS, tok), lambda i: (0, 0, 0)),
        out_shape=jax.ShapeDtypeStruct(bias.shape, BF),
        input_output_aliases={4: 0},
        compiler_params=pltpu.CompilerParams(vmem_limit_bytes=VMEM),
        name="gated_grad",
    )(core, cot, near, far, bias)


def slot_xor(t):
    return 2 * (t % 4) + t // 4


def attend_kernel(me_ref, bias_ref, q_ref, gate_ref, *refs):
    kv_refs = refs[:8]
    gated_ref, dq_ref, dgate_ref, dkv_own_ref, dkv_far_ref, dbias_ref = refs[8:14]
    s_scr, dp_scr = refs[14:]
    samples, _, tok = q_ref.shape
    head = pl.program_id(0)
    me = me_ref[0]
    scale = 1.0 / math.sqrt(HD)
    row_id = lax.broadcasted_iota(jnp.int32, (16, tok), 0)
    wanted = (row_id >= head * 3) & (row_id < head * 3 + 3)
    q = [q_ref[s] for s in range(samples)]
    sig, gg, gatt = [], [], []
    for s in range(samples):
        at = slice((s % 2) * 32, (s % 2) * 32 + 32)
        lanes = slice((s // 2) * 128, (s // 2) * 128 + 128)
        piece = bias_ref[:, at, lanes].astype(F32).reshape(tok, 128).T
        gg.append(jnp.where(head == 0, piece[:HD], piece[HD : 2 * HD]))
        sig.append(1.0 / (1.0 + jnp.exp(-gate_ref[s].astype(F32))))
        gatt.append((gg[s] * sig[s]).astype(BF))

    peak = [None] * samples
    for t in range(8):
        block = me ^ slot_xor(t)
        tops = bias_ref[block, TOP_AT:, :].astype(F32)
        top = jnp.sum(jnp.where(wanted, tops, 0.0), axis=0, keepdims=True)
        at = pl.ds(pl.multiple_of(GG_ROWS + head * 256, 64), 256)
        bias = bias_ref[block, at, :].astype(F32) + top
        for s in range(samples):
            score = mm(kv_refs[t][s, 0, :HD, :], q[s], TN) * scale + bias
            s_scr[s, t] = score
            high = jnp.max(score, axis=0, keepdims=True)
            peak[s] = high if t == 0 else jnp.maximum(peak[s], high)
    inv, dot = [], []
    for s in range(samples):
        total = jnp.zeros((1, tok), F32)
        weighted = jnp.zeros((1, tok), F32)
        for t in range(8):
            e = jnp.exp(s_scr[s, t] - peak[s])
            s_scr[s, t] = e
            dp = mm(kv_refs[t][s, 0, HD:, :], gatt[s], TN)
            dp_scr[s, t] = dp
            total = total + jnp.sum(e, axis=0, keepdims=True)
            weighted = weighted + jnp.sum(e * dp, axis=0, keepdims=True)
        inv.append(1.0 / total)
        dot.append(weighted * inv[s])
    pad = jnp.zeros((HD, tok), F32)
    pad2 = jnp.zeros((32, tok), F32)
    q_nat = [
        jnp.concatenate([q[s].astype(F32) * scale, pad, pad2], axis=0).T.astype(BF)
        for s in range(samples)
    ]
    g_nat = [
        jnp.concatenate([pad, gatt[s].astype(F32), pad2], axis=0).T.astype(BF)
        for s in range(samples)
    ]
    att = [jnp.zeros((HD, tok), F32)] * samples
    dq = [jnp.zeros((HD, tok), F32)] * samples
    for t in range(8):
        block = me ^ slot_xor(t)
        out_ref = dkv_own_ref if t < 4 else dkv_far_ref
        dbias = None
        for s in range(samples):
            prob = s_scr[s, t] * inv[s]
            prob_bf = prob.astype(BF)
            ds = prob * (dp_scr[s, t] - dot[s])
            dbias = ds if s == 0 else dbias + ds
            ds = ds.astype(BF)
            att[s] = att[s] + mm(kv_refs[t][s, 0, HD:, :], prob_bf, NN)
            dq[s] = dq[s] + mm(kv_refs[t][s, 0, :HD, :], ds, NN)
            dkv = mm(ds, q_nat[s], NN) + mm(prob_bf, g_nat[s], NN)
            out_ref[t % 4, s, 0] = dkv.T[: 2 * HD].astype(BF)
        dbias_ref[block, 0] = dbias.astype(BF)
    for s in range(samples):
        gated_ref[s] = (sig[s] * att[s]).astype(BF)
        dgate_ref[s] = (gg[s] * att[s] * sig[s] * (1.0 - sig[s])).astype(BF)
        dq_ref[s] = (dq[s] * scale).astype(BF)


def attend(me, bias, q, gate, kv):
    samples, feat, tok = q.shape
    heads = 2
    half = pl.BlockSpec((samples, HD, tok), lambda h: (0, h, 0))
    kv_spec = pl.BlockSpec((samples, 1, feat, tok), lambda h: (0, h, 0, 0))
    small = jax.ShapeDtypeStruct((samples, feat, tok), BF)
    dkv = jax.ShapeDtypeStruct((4, samples, heads, feat, tok), BF)
    dkv_spec = pl.BlockSpec((4, samples, 1, feat, tok), lambda h: (0, 0, h, 0, 0))
    return pl.pallas_call(
        attend_kernel,
        grid=(heads,),
        in_specs=[
            pl.BlockSpec(memory_space=pltpu.SMEM),
            pl.BlockSpec(bias.shape, lambda h: (0, 0, 0)),
            half,
            half,
        ]
        + [kv_spec] * 8,
        out_specs=[
            half,
            half,
            half,
            dkv_spec,
            dkv_spec,
            pl.BlockSpec((8, 1, 256, tok), lambda h: (0, h, 0, 0)),
        ],
        out_shape=[small, small, small, dkv, dkv, jax.ShapeDtypeStruct((8, heads, 256, tok), BF)],
        scratch_shapes=[pltpu.VMEM((samples, 8, 256, tok), F32)] * 2,
        compiler_params=pltpu.CompilerParams(vmem_limit_bytes=VMEM),
        cost_estimate=pl.CostEstimate(
            flops=2**34, bytes_accessed=20 * 2**20, transcendentals=2**22
        ),
        name="attend",
    )(me, bias, q, gate, *kv)


def fold_kernel(own_ref, far_ref, _, *out_refs):
    for k, out_ref in enumerate(out_refs):
        out_ref[...] = (own_ref[k].astype(F32) + far_ref[k].astype(F32)).astype(BF)


def fold(own, far, after):
    vmem = pl.BlockSpec(memory_space=pltpu.VMEM)
    return pl.pallas_call(
        fold_kernel,
        in_specs=[vmem, vmem, pl.BlockSpec(memory_space=pl.ANY)],
        out_shape=[jax.ShapeDtypeStruct(own.shape[1:], BF)] * own.shape[0],
        compiler_params=pltpu.CompilerParams(vmem_limit_bytes=VMEM),
        name="fold",
    )(own, far, after)


def norm_kernel(gated_ref, dq_ref, dg_ref, *refs):
    kv_refs = refs[:4]
    w_ref, part_ref, dcat_ref = refs[4:]
    dkv = kv_refs[0][0].astype(F32)
    for ref in kv_refs[1:]:
        dkv = dkv + ref[0].astype(F32)
    dkv = dkv.astype(BF)
    dcat = jnp.concatenate(
        [
            dq_ref[0],
            dkv[0, :HD],
            dkv[1, :HD],
            dkv[0, HD:],
            dkv[1, HD:],
            dg_ref[0],
        ],
        axis=0,
    )
    dcat_ref[0] = dcat
    cols, _, local, wide = part_ref.shape
    width = w_ref.shape[1]
    part = mm(dcat, w_ref[...], TN).astype(BF)
    part_ref[:, 0, :, :width] = part.reshape(cols, local, width)
    gated = jnp.concatenate([gated_ref[0], jnp.zeros((32, cols * local), BF)], axis=0)
    part_ref[:, 0, :, width:] = gated.astype(F32).T.astype(BF).reshape(cols, local, 128)


def norm_part(gated, dq, dg, kv_pieces, w_cat, cols):
    samples, feat, tok = dq.shape
    local = tok // cols
    all_feat, width = w_cat.shape
    half = pl.BlockSpec((1, feat, tok), lambda s: (s, 0, 0))
    kv_spec = pl.BlockSpec((1, 2, feat, tok), lambda s: (s, 0, 0, 0))
    return pl.pallas_call(
        norm_kernel,
        grid=(samples,),
        in_specs=[half, half, half]
        + [kv_spec] * 4
        + [pl.BlockSpec(w_cat.shape, lambda s: (0, 0))],
        out_specs=[
            pl.BlockSpec((cols, 1, local, width + 128), lambda s: (0, s, 0, 0)),
            pl.BlockSpec((1, all_feat, tok), lambda s: (s, 0, 0)),
        ],
        out_shape=[
            jax.ShapeDtypeStruct((cols, samples, local, width + 128), BF),
            jax.ShapeDtypeStruct((samples, all_feat, tok), BF),
        ],
        compiler_params=pltpu.CompilerParams(vmem_limit_bytes=VMEM),
        name="norm_part",
    )(gated, dq, dg, *kv_pieces, w_cat)


def weights_kernel(
    place_ref, dcat_ref, gated_ref, rows_ref, cot_ref, w_ref, gain_ref, grad_ref, gain_out_ref, acc
):
    step = pl.program_id(0)
    cols, local, width = rows_ref.shape
    dcat = dcat_ref[0]
    gated = gated_ref[0]
    grad = mm(dcat, rows_ref[...].reshape(cols * local, width), NN)
    grad_out = mm(gated, cot_ref[:, 0].reshape(cols * local, width), NN)
    four = dcat.shape[0]
    five = four + gated.shape[0]

    @pl.when(step == 0)
    def _():
        acc[:four, :] = grad
        acc[four:five, :] = grad_out
        acc[five:, :] = jnp.zeros((512 - five, width), F32)

    @pl.when(step > 0)
    def _():
        acc[:four, :] += grad
        acc[four:five, :] += grad_out

    @pl.when(step == pl.num_programs(0) - 1)
    def _():
        both = jnp.sum(acc[:four, :] * w_ref[...].astype(F32), axis=0, keepdims=True)
        gain_out_ref[...] = both / gain_ref[...]
        for p in range(8):
            grad_ref[p ^ place_ref[0]] = acc[p * 64 : (p + 1) * 64, :].astype(BF)


def weight_part(place, dcat, gated, rows_in, grad_rows, w_cat, gain):
    cols, samples, local, width = grad_rows.shape
    all_feat = w_cat.shape[0]
    feat, tok = gated.shape[1:]
    line = pl.BlockSpec((1, width), lambda s: (0, 0))
    return pl.pallas_call(
        weights_kernel,
        grid=(samples,),
        in_specs=[
            pl.BlockSpec(memory_space=pltpu.SMEM),
            pl.BlockSpec((1, all_feat, tok), lambda s: (s, 0, 0)),
            pl.BlockSpec((1, feat, tok), lambda s: (s, 0, 0)),
            pl.BlockSpec((cols, local, width), lambda s: (0, s, 0)),
            pl.BlockSpec((cols, 1, local, width), lambda s: (0, s, 0, 0)),
            pl.BlockSpec(w_cat.shape, lambda s: (0, 0)),
            line,
        ],
        out_specs=[pl.BlockSpec((8, 64, width), lambda s: (0, 0, 0)), line],
        out_shape=[
            jax.ShapeDtypeStruct((8, 64, width), BF),
            jax.ShapeDtypeStruct((1, width), F32),
        ],
        scratch_shapes=[pltpu.VMEM((512, width), F32)],
        compiler_params=pltpu.CompilerParams(vmem_limit_bytes=VMEM),
        name="weight_part",
    )(place, dcat, gated, rows_in, grad_rows, w_cat, gain)


def finish_kernel(core_ref, recv_ref, near_ref, far_ref, act_ref, cot_ref, gain_ref, out_ref, grad_ref):
    cols, samples, local, wide = recv_ref.shape
    width = act_ref.shape[-1]
    count = samples * local
    act = act_ref[...].reshape(count, width).astype(F32)
    cot = cot_ref[...].reshape(count, width).astype(F32)
    total = act
    grad_norm = jnp.zeros((count, width), F32)
    for c in range(cols):
        gated = recv_ref[c, :, :, width:].reshape(count, wide - width)[:, : 2 * HD]
        total = total + mm(gated, whole_w(near_ref[c], far_ref[c], core_ref[0]), NN)
        grad_norm = grad_norm + recv_ref[c, :, :, :width].reshape(count, width).astype(F32)
    out_ref[...] = total.astype(BF).reshape(samples, local, width)
    centred = act - jnp.mean(act, axis=-1, keepdims=True)
    inv_std = lax.rsqrt(jnp.mean(centred * centred, axis=-1, keepdims=True) + EPSILON)
    normed = centred * inv_std
    hat = grad_norm * gain_ref[...]
    back = inv_std * (
        hat
        - jnp.mean(hat, axis=-1, keepdims=True)
        - normed * jnp.mean(hat * normed, axis=-1, keepdims=True)
    )
    grad_ref[...] = (cot + back).astype(BF).reshape(samples, local, width)


def finish(core, recv, near, far, token_act, grad_out, gain):
    vmem = pl.BlockSpec(memory_space=pltpu.VMEM)
    return pl.pallas_call(
        finish_kernel,
        in_specs=[pl.BlockSpec(memory_space=pltpu.SMEM)] + [vmem] * 6,
        out_shape=[jax.ShapeDtypeStruct(token_act.shape, BF)] * 2,
        compiler_params=pltpu.CompilerParams(vmem_limit_bytes=VMEM),
        name="finish",
    )(core, recv, near, far, token_act, grad_out, gain)


def unpack_kernel(place_ref, near_ref, far_ref, *refs):
    outs, scr = refs[:5], refs[5]
    for p in range(4):
        slot = p ^ (place_ref[0] & 3)
        first = near_ref[slot].astype(F32)
        second = far_ref[slot].astype(F32)
        low = place_ref[0] < 4
        scr[p * 64 : (p + 1) * 64, :] = jnp.where(low, first, second)
        scr[256 + p * 64 : 256 + (p + 1) * 64, :] = jnp.where(low, second, first)
    feat = outs[4].shape[0]
    for k in range(5):
        outs[k][...] = scr[k * feat : (k + 1) * feat, :]


def unpack(place, near, far, feat):
    width = near.shape[-1]
    return pl.pallas_call(
        unpack_kernel,
        in_specs=[
            pl.BlockSpec(memory_space=pltpu.SMEM),
            pl.BlockSpec(memory_space=pltpu.VMEM),
            pl.BlockSpec(memory_space=pltpu.VMEM),
        ],
        out_shape=[jax.ShapeDtypeStruct((feat, width), F32)] * 5,
        scratch_shapes=[pltpu.VMEM((512, width), F32)],
        compiler_params=pltpu.CompilerParams(vmem_limit_bytes=16 * 2**20),
        name="unpack",
    )(place, near, far)


def wpair_kernel(db_ref, pair_ref, out_ref, db_scr, acc_ref):
    step = pair_ref.shape[0]
    chans = pair_ref.shape[2]
    heads = db_scr.shape[0]

    @pl.when(pl.program_id(0) == 0)
    def _():
        acc_ref[...] = jnp.zeros_like(acc_ref)

    for h in range(heads):
        db_scr[h] = db_ref[h // 2, h % 2].astype(F32).T.astype(BF)
    for block in range(step // 16):
        left = db_scr[:, block * 16 : (block + 1) * 16, :].reshape(heads * 16, db_scr.shape[2])
        for k in range(0, 16, 2):
            pair = jnp.concatenate(
                [pair_ref[block * 16 + k], pair_ref[block * 16 + k + 1]], axis=1
            )
            at = slice(k * chans, (k + 2) * chans)
            acc_ref[:, at] += mm(left, pair, NN)

    @pl.when(pl.program_id(0) == pl.num_programs(0) - 1)
    def _():
        total = jnp.zeros((heads, chans), F32)
        row_id = lax.broadcasted_iota(jnp.int32, (heads, 16, chans), 1)
        for k in range(16):
            piece = acc_ref[:, k * chans : (k + 1) * chans].reshape(heads, 16, chans)
            total = total + jnp.sum(jnp.where(row_id == k, piece, 0.0), axis=1)
        out_ref[...] = total


def wpair_part(dbias, pair):
    groups, per, keys, rows = dbias.shape
    heads = groups * per
    chans = pair.shape[2]
    step = 128
    return pl.pallas_call(
        wpair_kernel,
        grid=(rows // step,),
        in_specs=[
            pl.BlockSpec((groups, per, keys, step), lambda i: (0, 0, 0, i)),
            pl.BlockSpec((step, keys, chans), lambda i: (i, 0, 0)),
        ],
        out_specs=pl.BlockSpec((heads, chans), lambda i: (0, 0)),
        out_shape=jax.ShapeDtypeStruct((heads, chans), F32),
        scratch_shapes=[
            pltpu.VMEM((heads, step, keys), BF),
            pltpu.VMEM((heads * 16, 16 * chans), F32),
        ],
        compiler_params=pltpu.CompilerParams(vmem_limit_bytes=VMEM),
        cost_estimate=pl.CostEstimate(flops=2**32, bytes_accessed=20 * 2**20, transcendentals=0),
        name="wpair_part",
    )(dbias, pair)


def exchange(x, axes):
    return lax.all_to_all(x, axes, 0, 0, tiled=True)


def gather(x, axes, count):
    return exchange(jnp.broadcast_to(x[None], (count,) + x.shape), axes)


def swap(x, axis, count, k):
    return lax.ppermute(x, axis, [(i, i ^ k) for i in range(count)])


def add_bf(*terms):
    total = terms[0].astype(F32)
    for term in terms[1:]:
        total = total + term.astype(F32)
    return total.astype(BF)


def add_four(x, axes):
    one, two, three = (swap(x, axes, 4, k) for k in range(1, 4))
    return (x + one) + (two + three)


def on_device(
    token_act, pair_rep, norm_gain, w_pair, w_query, w_key, w_value, w_gate, w_out, grad_out
):
    samples, local, width = token_act.shape
    feat = w_out.shape[0]
    cols = 8
    count = samples * local
    y, core, smp = (lax.axis_index(name) for name in ("y", "core", "smp"))
    me = jnp.full((1,), y * 2 + core, jnp.int32)
    which = jnp.full((1,), core, jnp.int32)
    place = jnp.full((1,), core * 4 + y, jnp.int32)

    load = prepare(which, token_act, norm_gain, w_out, cols)
    rows_in = exchange(load, COL)
    bias, cot_load = pair_bias(pair_rep, w_pair, grad_out)
    rows_in, bias = lax.optimization_barrier((rows_in, bias))
    w_near = rows_in[:, count:]
    w_far = swap(w_near, "core", 2, 1)
    bias = gated_grad(which, grad_out.reshape(count, width), w_near, w_far, bias)
    bias = exchange(bias, COL)

    grad_rows = exchange(cot_load, COL)

    wq, wk, wv, wg = w_query.T, w_key.T, w_value.T, w_gate.T
    q, kv_own, gate = project(rows_in, samples, local, wq, wk, wv, wg)
    near = [kv_own] + [swap(kv_own, "y", 4, k) for k in range(1, 4)]
    far = [swap(x, "core", 2, 1) for x in near]

    gated, dq, dgate, dkv_own, dkv_far, dbias = attend(me, bias, q, gate, near + far)
    dbias = exchange(dbias, COL)
    dkv = fold(dkv_own, swap(dkv_far, "core", 2, 1), grad_rows)
    pieces = [dkv[0]] + [swap(dkv[k], "y", 4, k) for k in range(1, 4)]
    w_cat = jnp.concatenate([wq, wk, wv, wg], axis=0)
    part, dcat = norm_part(gated, dq, dgate, pieces, w_cat, cols)
    recv = exchange(part, COL)
    blocks, gain_part = weight_part(
        place, dcat, gated, rows_in, grad_rows, w_cat, norm_gain[None, :]
    )

    blocks = add_bf(blocks[:4], swap(blocks[4:], "core", 2, 1))
    mine = add_bf(blocks[0], *(swap(blocks[k], "y", 4, k) for k in range(1, 4)))
    wpair = wpair_part(dbias, pair_rep)
    tiny = jnp.concatenate([wpair.reshape(16, 128), gain_part.reshape(6, 128)], axis=0)
    tiny = add_four(tiny, "y")
    tiny = tiny + swap(tiny, "core", 2, 1)

    tiny, mine, recv = lax.optimization_barrier((tiny, mine, recv))
    mine = add_bf(mine, swap(mine, "smp", 2, 1))
    tiny = jnp.sum(gather(tiny, COL + ("smp",), 16), axis=0)
    quad = jnp.stack([mine] + [swap(mine, "y", 4, k) for k in range(1, 4)])
    grads = unpack(place, quad, swap(quad, "core", 2, 1), feat)
    grads = [x.T for x in grads[:4]] + [grads[4]]

    block_out, grad_act = finish(
        which, recv, w_near, w_far, token_act, grad_out, norm_gain[None, :]
    )
    return (block_out, grad_act, *grads, tiny[:16].T, tiny[16:].reshape(width))


def solution(mesh):
    fine = Mesh(mesh.devices.reshape(4, 2, 4, 2, 2), ("y", "core", "z", "xh", "smp"))
    tokens = P("smp", ROW + COL, None)
    split_last = P(None, COL)
    return jax.shard_map(
        on_device,
        mesh=fine,
        in_specs=(
            tokens,
            P(ROW, COL, None),
            P(),
            P(),
            split_last,
            split_last,
            split_last,
            split_last,
            P(COL, None),
            tokens,
        ),
        out_specs=(
            tokens,
            tokens,
            split_last,
            split_last,
            split_last,
            split_last,
            P(COL, None),
            P(),
            P(),
        ),
        check_vma=False,
    )
```
